512 devices in a mesh: rows: 64 (over z_lo, x, y), aggs: 4 (over z_hi), vecs: 2 (over core).
Axes of the slice: x: 4, y: 4, z: 16 (z_hi: 4, z_lo: 4; z = z_hi * 4 + z_lo), core: 2. Of those that a mesh axis runs over, the one named last changes fastest.
Arguments:
- couplings: bfloat16 [1024, 8, 192, 192], P('rows', 'aggs'), may hold values from -0.19921875 to 0.19921875
- diag_blocks: bfloat16 [1024, 192, 192], P('rows'), may hold values from -0.201 to 3, as said below
- coupling_cols: int32 [1024, 8], P('rows', 'aggs'), may hold values from 0 to 1023, as said below
- aggregate: int32 [1024], P('rows'), may hold values from 0 to 511, as said below
- pattern: int32 [1024, 3], P('rows'), may hold values from 0 to 511, as said below
- tests: float32 [1024, 32, 192], P('rows', 'vecs'), may hold values from -6 to 6
Outputs:
- prolongator: bfloat16 [1024, 4, 32, 192], P('rows', 'aggs', 'vecs')
- coarse: float32 [512, 24, 32, 32], P('rows', 'aggs', 'vecs')
The draws below stay inside these ranges and needn't reach their ends.
Inputs may be any that keep to these rules, and one draw needn't show every extreme that they name: `diag_blocks`: Off-diagonal entries of each block lie within about 0.2 of zero; the diagonal entries lie between 1 and 3. `coupling_cols`: the columns of a block row are distinct, none equals the row, and each lies in the row's own slab of 16 block rows or in the slab just before or after it. A block row of slab s belongs to one of the aggregates s * 8 to s * 8 + 7, and every aggregate has one block row or more. `pattern`: the entries of a row are distinct aggregates of the row's own slab, none equal to the row's aggregate.
All inputs are finite; a program needn't handle non-finite values.
Results may differ from the reference program's by a relative error of at most 0.009.
Values may be sent and summed in bfloat16 or wider, within the bound.
No kernel may reach another device: no remote copies, remote signals or barrier semaphores. Data moves between devices by JAX's collectives and lax.ppermute only.
A program may use at most 64 MiB of HBM per device.

```python
import math
import jax
import jax.numpy as jnp
from jax import lax

BLOCK = 192
VECTORS = 32
COUPLED = 8
SLOTS = 4
SWEEPS = 3
SLAB_ROWS = 16
SLAB_AGGS = 8
BLOCK_ROWS = 1024
N_ROWS = 64


def grouping(key):
    slab_count = BLOCK_ROWS // SLAB_ROWS
    slab_keys = jax.random.split(key, slab_count)

    def per_slab(slab_key):
        first_key, second_key = jax.random.split(slab_key)
        ranking = jax.random.permutation(first_key, SLAB_ROWS)
        spare_ids = jax.random.randint(second_key, (SLAB_ROWS,), 0, SLAB_AGGS)
        return jnp.where(ranking < SLAB_AGGS, ranking, spare_ids).astype(jnp.int32)
    local_ids = jax.vmap(per_slab)(slab_keys)
    offsets = (jnp.arange(slab_count, dtype=jnp.int32) * SLAB_AGGS)[:, None]
    return (local_ids + offsets).reshape(BLOCK_ROWS).astype(jnp.int32)


def draw_aggregate(key, part):
    return grouping(key)


def draw_pattern(key, part):
    owners = grouping(key)
    key = jax.random.fold_in(key, 12)
    row_ids = jnp.arange(BLOCK_ROWS, dtype=jnp.int32)
    offsets = row_ids // SLAB_ROWS * SLAB_AGGS
    positions = jnp.arange(SLAB_AGGS, dtype=jnp.int32)
    scores = jax.random.randint(key, (BLOCK_ROWS, SLAB_AGGS), 0, 4096) * SLAB_AGGS + positions[None, :]
    scores = jnp.where(positions[None, :] == (owners - offsets)[:, None], -1, scores)
    picked = lax.top_k(scores, SLOTS - 1)[1].astype(jnp.int32)
    return (picked + offsets[:, None]).astype(jnp.int32)


def draw_coupling_cols(key, part):
    key = jax.random.fold_in(key, 13)
    span_width = 3 * SLAB_ROWS
    row_ids = jnp.arange(BLOCK_ROWS, dtype=jnp.int32)
    window_start = (row_ids // SLAB_ROWS - 1) * SLAB_ROWS
    positions = jnp.arange(span_width, dtype=jnp.int32)
    candidates = window_start[:, None] + positions[None, :]
    allowed = (candidates >= 0) & (candidates < BLOCK_ROWS) & (candidates != row_ids[:, None])
    scores = jax.random.randint(key, (BLOCK_ROWS, span_width), 0, 4096) * span_width + positions[None, :]
    scores = jnp.where(allowed, scores, -1)
    picked = lax.top_k(scores, COUPLED)[1].astype(jnp.int32)
    return (window_start[:, None] + picked).astype(jnp.int32)


def draw_diag_blocks(key, part):
    key = jax.random.fold_in(key, 14)
    first_key, second_key = jax.random.split(key)
    spread = jax.random.normal(first_key, (BLOCK_ROWS, BLOCK, BLOCK)) * 0.035
    pivots = jnp.exp(jax.random.uniform(second_key, (BLOCK_ROWS, BLOCK), minval=0.0, maxval=math.log(3.0)))
    identity = jnp.eye(BLOCK, dtype=jnp.float32)
    spread = jnp.clip(spread, -0.2, 0.2)
    return (spread * (1.0 - identity) + identity * pivots[:, :, None]).astype(jnp.bfloat16)


def level_of(own_key, shape, cuts, low, high):
    def one(axis_at, shards_of):
        heights = jax.random.uniform(jax.random.fold_in(jax.random.fold_in(own_key, 6), axis_at), (shards_of,), jnp.float32, low / len(cuts), high / len(cuts))
        return jnp.repeat(jnp.exp(heights), shape[axis_at] // shards_of).reshape((-1,) + (1,) * (len(shape) - axis_at - 1))

    level = one(*cuts[0])
    for cut in cuts[1:]:
        level = level * one(*cut)
    return level


def gaussian(stream_key, dims, scale, limit, cuts=(), kind=jnp.bfloat16):
    result = jax.random.normal(stream_key, dims, jnp.float32) * scale
    if len(cuts) > 0:
        result = level_of(stream_key, dims, cuts, -0.22, 0.18) * result
    return jnp.clip(result, min=-limit, max=limit).astype(kind)


def setup_inputs(seed: int = 0) -> dict:
    splits = jax.random.split(jax.random.key(seed), 7)
    return {
        "couplings": gaussian(splits[0], (BLOCK_ROWS, COUPLED, BLOCK, BLOCK), 0.035, 0.19921875, ((0, 64), (1, 4))),
        "diag_blocks": draw_diag_blocks(jax.random.fold_in(splits[6], 71), 0),
        "coupling_cols": draw_coupling_cols(jax.random.fold_in(splits[6], 71), 0),
        "aggregate": draw_aggregate(jax.random.fold_in(splits[6], 71), 0),
        "pattern": draw_pattern(jax.random.fold_in(splits[6], 71), 0),
        "tests": gaussian(splits[5], (BLOCK_ROWS, VECTORS, BLOCK), 1.0, 6.0, ((0, 64), (1, 2)), jnp.float32),
    }


DAMPING = 2.0 / 3.0
HIGHEST_PRECISION = lax.Precision.HIGHEST

def by_slab(values):
    return values.reshape((N_ROWS, SLAB_ROWS) + values.shape[1:])

def flatten_slabs(values):
    return values.reshape((N_ROWS * SLAB_ROWS,) + values.shape[2:])

def rounded_back(values):
    return lax.optimization_barrier(values.astype(jnp.bfloat16)).astype(jnp.float32)

def apply_stiffness(couplings, diag_blocks, coupling_cols, rounded):

    def per_slab(pieces):
        blocks, center, columns, own_rows = pieces
        nearby = rounded[columns].astype(jnp.float32)
        partial_sum = jnp.einsum('ikab,ikvb->iva', blocks.astype(jnp.float32), nearby, precision=HIGHEST_PRECISION)
        return partial_sum + jnp.einsum('iab,ivb->iva', center.astype(jnp.float32), own_rows.astype(jnp.float32), precision=HIGHEST_PRECISION)
    return flatten_slabs(lax.map(per_slab, (by_slab(couplings), by_slab(diag_blocks), by_slab(coupling_cols), by_slab(rounded))))

def reference(couplings, diag_blocks, coupling_cols, aggregate, pattern, tests):
    pivots = jnp.diagonal(diag_blocks, axis1=1, axis2=2).astype(jnp.float32)
    current = tests
    for sweep_index in range(SWEEPS):
        rounded = current.astype(jnp.bfloat16)
        product = apply_stiffness(couplings, diag_blocks, coupling_cols, rounded)
        current = current - DAMPING * product / pivots[:, None, :]
    grams_rows = jnp.einsum('ivb,iwb->ivw', current, current, precision=HIGHEST_PRECISION)
    totals = jax.ops.segment_sum(grams_rows, aggregate, num_segments=N_ROWS * SLAB_AGGS) / BLOCK
    factor_low = jnp.linalg.cholesky(totals)
    identity = jnp.broadcast_to(jnp.eye(VECTORS, dtype=jnp.float32), totals.shape)
    inverse = lax.linalg.triangular_solve(factor_low, identity, left_side=True, lower=True)
    tentative = jnp.einsum('icv,ivb->icb', inverse[aggregate], current, precision=HIGHEST_PRECISION)
    tentative_b = tentative.astype(jnp.bfloat16)
    slot_aggs = jnp.concatenate([aggregate[:, None], pattern], axis=1)
    leading = (jnp.arange(SLOTS, dtype=jnp.int32) == 0).astype(jnp.float32)

    def fitting(pieces):
        blocks, center, columns, own_slots, own_tent, own_tent_b, own_pivots = pieces
        moved_rows = jnp.einsum('ikab,ikcb->ikca', blocks.astype(jnp.float32), tentative_b[columns].astype(jnp.float32), precision=HIGHEST_PRECISION)
        matches = (aggregate[columns][:, :, None] == own_slots[:, None, :]).astype(jnp.float32)
        partials = jnp.einsum('ikp,ikca->ipca', matches, moved_rows, precision=HIGHEST_PRECISION)
        center_fit = jnp.einsum('iab,icb->ica', center.astype(jnp.float32), own_tent_b.astype(jnp.float32), precision=HIGHEST_PRECISION)
        partials = partials + leading[None, :, None, None] * center_fit[:, None]
        return leading[None, :, None, None] * own_tent[:, None] - DAMPING * partials / own_pivots[:, None, None, :]
    fitted = flatten_slabs(lax.map(fitting, (by_slab(couplings), by_slab(diag_blocks), by_slab(coupling_cols), by_slab(slot_aggs), by_slab(tentative), by_slab(tentative_b), by_slab(pivots))))
    prolongator = fitted.astype(jnp.bfloat16)
    span_width = 3 * SLAB_AGGS

    def galerkin(pieces):
        slab_index, blocks, center, columns, own_slots, own_prolong = pieces
        nearby = prolongator[columns].astype(jnp.float32)
        reached = rounded_back(jnp.einsum('ikxy,ikqey->ikqex', blocks.astype(jnp.float32), nearby, precision=HIGHEST_PRECISION))
        own_float = own_prolong.astype(jnp.float32)
        center_reach = rounded_back(jnp.einsum('ixy,iqey->iqex', center.astype(jnp.float32), own_float, precision=HIGHEST_PRECISION))
        crossed = jnp.einsum('ipdx,ikqex->ikpqde', own_float, reached, precision=HIGHEST_PRECISION)
        center_cross = jnp.einsum('ipdx,iqex->ipqde', own_float, center_reach, precision=HIGHEST_PRECISION)
        row_hot = ((own_slots - slab_index * SLAB_AGGS)[:, :, None] == jnp.arange(SLAB_AGGS, dtype=jnp.int32)).astype(jnp.float32)
        column_base = (slab_index - 1) * SLAB_AGGS
        col_hot = ((slot_aggs[columns] - column_base)[..., None] == jnp.arange(span_width, dtype=jnp.int32)).astype(jnp.float32)
        center_hot = ((own_slots - column_base)[..., None] == jnp.arange(span_width, dtype=jnp.int32)).astype(jnp.float32)
        coarse_part = jnp.einsum('ipg,ikqn,ikpqde->gnde', row_hot, col_hot, crossed, precision=HIGHEST_PRECISION)
        coarse_part = coarse_part + jnp.einsum('ipg,iqn,ipqde->gnde', row_hot, center_hot, center_cross, precision=HIGHEST_PRECISION)
        return coarse_part / BLOCK
    slab_ids = jnp.arange(N_ROWS, dtype=jnp.int32)
    coarse = lax.map(galerkin, (slab_ids, by_slab(couplings), by_slab(diag_blocks), by_slab(coupling_cols), by_slab(slot_aggs), by_slab(prolongator)))
    coarse = coarse.reshape((N_ROWS * SLAB_AGGS, span_width, VECTORS, VECTORS))
    return (prolongator, coarse)
```

```python
import functools

import jax
import jax.numpy as jnp
from jax import lax
from jax.experimental import pallas as pl
from jax.experimental.pallas import tpu as pltpu
from jax.sharding import PartitionSpec as P

VECTORS = 32
SWEEPS = 3
SLAB_AGGS = 8
SLOTS = 4
DAMPING = 2.0 / 3.0
HIGHEST_PRECISION = lax.Precision.HIGHEST
BF16 = jnp.bfloat16
F32 = jnp.float32
VMEM_LIMIT = 32 * 1024 * 1024

SMEM_SPEC = pl.BlockSpec(memory_space=pltpu.SMEM)
VMEM_SPEC = pl.BlockSpec(memory_space=pltpu.VMEM)


def dot_nt(left, right):
    return lax.dot_general(left, right, (((1,), (1,)), ((), ())), preferred_element_type=F32)


def params():
    return pltpu.CompilerParams(vmem_limit_bytes=VMEM_LIMIT)


def center_kernel(diag_ref, x_ref, scale_ref, y_ref):
    for i in range(x_ref.shape[0]):
        x = x_ref[i]
        y_ref[i] = x - scale_ref[i : i + 1, :] * dot_nt(x.astype(BF16), diag_ref[i])


def first_center_kernel(diag_ref, x_ref, y_ref, scale_ref):
    width = x_ref.shape[2]
    on_diagonal = lax.broadcasted_iota(jnp.int32, (width, width), 0) == lax.broadcasted_iota(
        jnp.int32, (width, width), 1
    )
    for i in range(x_ref.shape[0]):
        x = x_ref[i]
        block = diag_ref[i]
        pivot = jnp.sum(jnp.where(on_diagonal, block.astype(F32), 0.0), axis=0, keepdims=True)
        scale = DAMPING / pivot
        scale_ref[i : i + 1, :] = scale
        y_ref[i] = x - scale * dot_nt(x.astype(BF16), block)


def couple_kernel(col_ref, a_ref, before_ref, own_ref, after_ref, out_ref, ext):
    rows, stored = a_ref.shape[:2]
    ext[0:rows] = before_ref[...]
    ext[rows : 2 * rows] = own_ref[...]
    ext[2 * rows : 3 * rows] = after_ref[...]
    for i in range(rows):
        total = dot_nt(ext[col_ref[i, 0]], a_ref[i, 0])
        for k in range(1, stored):
            total = total + dot_nt(ext[col_ref[i, k]], a_ref[i, k])
        out_ref[i] = total.astype(BF16)


def fit_kernel(col_ref, a_ref, own_ref, out_ref):
    rows, stored = a_ref.shape[:2]
    for i in range(rows):
        for k in range(stored):
            row = jnp.clip(col_ref[i, k] - rows, 0, rows - 1)
            out_ref[i, k] = dot_nt(own_ref[row], a_ref[i, k]).astype(BF16)


def slot_kernel(slot_ref, far_slot_ref, near_ref, far_ref, out_ref):
    rows, stored = near_ref.shape[:2]
    for i in range(rows):
        for p in range(SLOTS):
            total = jnp.zeros(near_ref.shape[2:], F32)
            for k in range(stored):
                total = total + jnp.where(slot_ref[i, k] == p, near_ref[i, k].astype(F32), 0.0)
                total = total + jnp.where(far_slot_ref[i, k] == p, far_ref[i, k].astype(F32), 0.0)
            out_ref[i, p] = total.astype(BF16)


def inverse_factor_kernel(m_ref, out_ref):
    size = m_ref.shape[0]
    rows = [m_ref[v] for v in range(size)]
    place = lax.broadcasted_iota(jnp.int32, rows[0].shape, 0)
    for k in range(size):
        root = lax.rsqrt(rows[k][k : k + 1, :])
        here = place == k
        pivot_row = jnp.where(here, root, rows[k] * root)
        rows[k] = jnp.where(place <= k, pivot_row, 0.0)
        out_ref[k] = rows[k]
        for v in range(k + 1, size):
            rows[v] = jnp.where(here, 0.0, rows[v]) - pivot_row[v : v + 1, :] * pivot_row


def coarse_kernel(
    where_ref, col_ref, place_ref, a_ref, diag_ref, before_ref, own_ref, after_ref, other_ref,
    keep_ref, send_ref, ext, reach, left, total,
):
    rows, stored = a_ref.shape[:2]
    vectors = own_ref.shape[2]
    width = own_ref.shape[3]
    share = rows // 4
    core, slot = where_ref[0], where_ref[1]
    ext[0:rows] = before_ref[...]
    ext[rows : 2 * rows] = own_ref[...]
    ext[2 * rows : 3 * rows] = after_ref[...]
    reach[...] = jnp.zeros_like(reach)
    left[...] = jnp.zeros_like(left)
    span = reach.shape[1]

    def add(i, row, block):
        image = dot_nt(ext[row].reshape(SLOTS * vectors, width), block)
        for q in range(SLOTS):
            at = place_ref[row, q]
            reach[i, at] = reach[i, at] + image[q * vectors : (q + 1) * vectors]

    for i in range(rows):
        for p in range(SLOTS):
            group = place_ref[rows + i, p] - SLAB_AGGS
            left[i, group, core] = own_ref[i, p]
            left[i, group, 1 - core] = other_ref[i, p]
        for k in range(stored):
            add(i, col_ref[i, k], a_ref[i, k])

    for r in range(share):
        i = slot * share + r
        add(i, rows + i, diag_ref[i])

    for i in range(rows):
        product = dot_nt(
            reach[i].astype(BF16).reshape(span * vectors, width),
            left[i].reshape(SLAB_AGGS * 2 * vectors, width),
        )
        if i == 0:
            total[...] = product
        else:
            total[...] = total[...] + product
    quarter = span * vectors // 4
    for n in range(2):
        start = pl.multiple_of(where_ref[2 + n] * quarter, 32)
        keep_ref[n] = total[pl.ds(start, quarter), :] * (1.0 / width)
        start = pl.multiple_of(where_ref[4 + n] * quarter, 32)
        send_ref[n] = (total[pl.ds(start, quarter), :] * (1.0 / width)).astype(BF16)


def shift(x, by):
    size = lax.axis_size("rows")
    return lax.ppermute(x, "rows", [(i, i + by) for i in range(size) if 0 <= i + by < size])


def partner(slot, core, phase):
    return slot ^ 1 if (core + phase) % 2 == 0 else 3 - slot


def exchange(x, phase):
    pairs = [(2 * s + c, 2 * partner(s, c, phase) + c) for s in range(4) for c in range(2)]
    return lax.ppermute(x, ("aggs", "vecs"), pairs)


def on_device(couplings, diag_blocks, coupling_cols, aggregate, pattern, tests):
    rows, vectors, width = tests.shape
    stored = couplings.shape[1]
    slab = lax.axis_index("rows")
    slot = lax.axis_index("aggs")
    core = lax.axis_index("vecs")
    shape = (rows, vectors, width)
    cols = coupling_cols - slab * rows + rows

    local_aggs = aggregate - slab * SLAB_AGGS
    slot_aggs = jnp.concatenate([aggregate[:, None], pattern], axis=1) - slab * SLAB_AGGS
    before_slots = shift(slot_aggs, 1)
    after_slots = shift(slot_aggs, -1)
    places = jnp.concatenate(
        [before_slots, slot_aggs + SLAB_AGGS, after_slots + 2 * SLAB_AGGS], axis=0
    )

    def slots_of(columns):
        inside = columns[:, :, None] == jnp.arange(rows, 2 * rows, dtype=jnp.int32)
        aggs = jnp.sum(jnp.where(inside, local_aggs + 1, 0), axis=2) - 1
        hits = aggs[:, :, None] == slot_aggs[:, None, :]
        return jnp.sum(jnp.where(hits, jnp.arange(1, SLOTS + 1, dtype=jnp.int32), 0), axis=2) - 1

    near_slot = slots_of(cols)
    far_slot = exchange(near_slot, 0)

    center = pl.pallas_call(
        center_kernel,
        out_shape=jax.ShapeDtypeStruct(shape, F32),
        in_specs=[VMEM_SPEC] * 3,
        out_specs=VMEM_SPEC,
        compiler_params=params(),
        name="center",
    )
    first_center = pl.pallas_call(
        first_center_kernel,
        out_shape=[jax.ShapeDtypeStruct(shape, F32), jax.ShapeDtypeStruct((rows, width), F32)],
        in_specs=[VMEM_SPEC] * 2,
        out_specs=[VMEM_SPEC] * 2,
        compiler_params=params(),
        name="first_center",
    )
    couple = pl.pallas_call(
        couple_kernel,
        out_shape=jax.ShapeDtypeStruct(shape, BF16),
        in_specs=[SMEM_SPEC] + [VMEM_SPEC] * 4,
        out_specs=VMEM_SPEC,
        scratch_shapes=[pltpu.VMEM((3 * rows, vectors, width), BF16)],
        compiler_params=params(),
        name="couple",
    )

    current = tests
    scale = None
    for sweep in range(SWEEPS):
        rounded = current.astype(BF16)
        before = shift(rounded, 1)
        after = shift(rounded, -1)
        if sweep == 0:
            rest, scale = first_center(diag_blocks, current)
        else:
            rest = center(diag_blocks, current, scale)
        part = couple(cols, couplings, before, rounded, after)
        pair = (part.astype(F32) + exchange(part, 0).astype(F32)).astype(BF16)
        whole = pair.astype(F32) + exchange(pair, 1).astype(F32)
        current = rest - scale[:, None, :] * whole

    every = lax.all_gather(current, "vecs", axis=1, tiled=True)
    grams = jnp.einsum("ivb,iwb->ivw", every, every, precision=HIGHEST_PRECISION)
    members = (local_aggs[:, None] == jnp.arange(SLAB_AGGS, dtype=jnp.int32)[None, :]).astype(F32)
    totals = jnp.einsum("ig,ivw->vwg", members, grams, precision=HIGHEST_PRECISION) / width
    inverse = pl.pallas_call(
        inverse_factor_kernel,
        out_shape=jax.ShapeDtypeStruct((VECTORS, VECTORS, SLAB_AGGS), F32),
        in_specs=[VMEM_SPEC],
        out_specs=VMEM_SPEC,
        compiler_params=params(),
        name="inverse_factor",
    )(totals)
    own_inverse = lax.dynamic_slice_in_dim(inverse, core * vectors, vectors, 0)
    row_inverse = jnp.einsum("ig,cvg->icv", members, own_inverse, precision=HIGHEST_PRECISION)
    tentative = jnp.einsum("icv,ivb->icb", row_inverse, every, precision=HIGHEST_PRECISION)

    moved = pl.pallas_call(
        fit_kernel,
        out_shape=jax.ShapeDtypeStruct((rows, stored, vectors, width), BF16),
        in_specs=[SMEM_SPEC] + [VMEM_SPEC] * 2,
        out_specs=VMEM_SPEC,
        compiler_params=params(),
        name="fit",
    )(cols, couplings, tentative.astype(BF16))
    rest = center(diag_blocks, tentative, scale)
    far_moved = exchange(moved, 0)
    pair = pl.pallas_call(
        slot_kernel,
        out_shape=jax.ShapeDtypeStruct((rows, SLOTS, vectors, width), BF16),
        in_specs=[SMEM_SPEC] * 2 + [VMEM_SPEC] * 2,
        out_specs=VMEM_SPEC,
        compiler_params=params(),
        name="slots",
    )(near_slot, far_slot, moved, far_moved)
    fitted = pair.astype(F32) + exchange(pair, 1).astype(F32)
    leading = (jnp.arange(SLOTS, dtype=jnp.int32) == 0)[None, :, None, None]
    prolong = (
        jnp.where(leading, rest[:, None], 0.0) - scale[:, None, None, :] * fitted
    ).astype(BF16)
    prolong_here = lax.dynamic_slice_in_dim(prolong, slot, 1, 1)

    before = shift(prolong, 1)
    after = shift(prolong, -1)
    other = lax.ppermute(prolong, "vecs", [(0, 1), (1, 0)])
    first = jnp.where(core == 0, slot ^ 1, 3 - slot)
    second = jnp.where(core == 0, 3 - slot, slot ^ 1)
    where = jnp.stack([core, slot, slot, second, first, slot ^ 2]).astype(jnp.int32)
    span = 3 * SLAB_AGGS
    quarter = span * vectors // 4
    wide = SLAB_AGGS * 2 * vectors
    keep, send = pl.pallas_call(
        coarse_kernel,
        out_shape=[
            jax.ShapeDtypeStruct((2, quarter, wide), F32),
            jax.ShapeDtypeStruct((2, quarter, wide), BF16),
        ],
        in_specs=[SMEM_SPEC] * 3 + [VMEM_SPEC] * 6,
        out_specs=[VMEM_SPEC] * 2,
        scratch_shapes=[
            pltpu.VMEM((3 * rows, SLOTS, vectors, width), BF16),
            pltpu.VMEM((rows, span, vectors, width), F32),
            pltpu.VMEM((rows, SLAB_AGGS, 2, vectors, width), BF16),
            pltpu.VMEM((span * vectors, wide), F32),
        ],
        compiler_params=params(),
        name="coarse",
    )(where, cols, places, couplings, diag_blocks, before, prolong, after, other)
    half = keep + exchange(send, 0).astype(F32)
    owned = half[0] + exchange(half[1].astype(BF16), 1).astype(F32)
    owned = owned.reshape(span // 4, vectors, SLAB_AGGS, 2, vectors)
    mine = lax.dynamic_index_in_dim(owned, core, 3, keepdims=False)
    theirs = lax.dynamic_index_in_dim(owned, 1 - core, 3, keepdims=False)
    theirs = lax.ppermute(theirs, "vecs", [(0, 1), (1, 0)])
    low = jnp.where(core == 0, mine, theirs)
    high = jnp.where(core == 0, theirs, mine)
    coarse = jnp.concatenate([low, high], axis=1).transpose(2, 0, 3, 1)
    return (prolong_here, coarse)


def solution(mesh):
    return jax.shard_map(
        on_device,
        mesh=mesh,
        in_specs=(
            P("rows", "aggs", None, None),
            P("rows", None, None),
            P("rows", "aggs"),
            P("rows"),
            P("rows", None),
            P("rows", "vecs", None),
        ),
        out_specs=(P("rows", "aggs", "vecs", None), P("rows", "aggs", "vecs", None)),
        check_vma=False,
    )
```

```python
import jax
import jax.numpy as jnp
from jax import lax
from jax.experimental import pallas as pl
from jax.experimental.pallas import tpu as pltpu
from jax.sharding import PartitionSpec as P

VECTORS = 32
SWEEPS = 3
SLAB_AGGS = 8
SLOTS = 4
DAMPING = 2.0 / 3.0
HIGHEST_PRECISION = lax.Precision.HIGHEST
BF16 = jnp.bfloat16
F32 = jnp.float32

SMEM_SPEC = pl.BlockSpec(memory_space=pltpu.SMEM)
VMEM_SPEC = pl.BlockSpec(memory_space=pltpu.VMEM)


def dot_nt(left, right):
    return lax.dot_general(left, right, (((1,), (1,)), ((), ())), preferred_element_type=F32)


def center_kernel(diag_ref, x_ref, scale_ref, y_ref):
    for i in range(x_ref.shape[0]):
        x = x_ref[i]
        y_ref[i] = x - scale_ref[i : i + 1, :] * dot_nt(x.astype(BF16), diag_ref[i])


def first_center_kernel(diag_ref, x_ref, y_ref, scale_ref):
    width = x_ref.shape[2]
    on_diagonal = lax.broadcasted_iota(jnp.int32, (width, width), 0) == lax.broadcasted_iota(
        jnp.int32, (width, width), 1
    )
    for i in range(x_ref.shape[0]):
        x = x_ref[i]
        block = diag_ref[i]
        pivot = jnp.sum(jnp.where(on_diagonal, block.astype(F32), 0.0), axis=0, keepdims=True)
        scale = DAMPING / pivot
        scale_ref[i : i + 1, :] = scale
        y_ref[i] = x - scale * dot_nt(x.astype(BF16), block)


def fold_kernel(x_ref, out_ref):
    rows, _, width = x_ref.shape
    for m in range(rows // 2):
        out_ref[m, :, :width] = x_ref[m].astype(BF16)
        out_ref[m, :, width:] = x_ref[rows // 2 + m].astype(BF16)


def update_kernel(rest_ref, near_ref, far_ref, scale_ref, *refs):
    rows, _, width = rest_ref.shape
    half = rows // 2
    extra_ref = refs[0] if len(refs) == 3 else None
    x_ref, folded_ref = refs[-2:]
    for m in range(half):
        total = near_ref[m].astype(F32) + far_ref[m].astype(F32)
        low = rest_ref[m] - scale_ref[m : m + 1, :] * total[:, :width]
        high = rest_ref[half + m] - scale_ref[half + m : half + m + 1, :] * total[:, width:]
        x_ref[m] = low
        x_ref[half + m] = high
        folded_ref[m, :, :width] = low.astype(BF16)
        folded_ref[m, :, width:] = high.astype(BF16)
    if extra_ref is not None:
        folded_ref[half] = extra_ref[...]


def couple_kernel(col_ref, a_ref, before_ref, own_ref, after_ref, *refs):
    rows, stored, width = a_ref.shape[:3]
    half = rows // 2
    extra_ref = refs[0] if len(refs) == 3 else None
    out_ref, ext = refs[-2:]
    for s, ref in enumerate((before_ref, own_ref, after_ref)):
        for m in range(half):
            block = ref[m]
            ext[s * rows + m] = block[:, :width]
            ext[s * rows + half + m] = block[:, width:]

    def product(i):
        total = dot_nt(ext[col_ref[i, 0]], a_ref[i, 0])
        for k in range(1, stored):
            total = total + dot_nt(ext[col_ref[i, k]], a_ref[i, k])
        return total.astype(BF16)

    for m in range(half):
        out_ref[m, :, :width] = product(m)
        out_ref[m, :, width:] = product(half + m)
    if extra_ref is not None:
        out_ref[half] = extra_ref[...]


def fit_kernel(col_ref, a_ref, own_ref, out_ref):
    rows, stored, width = a_ref.shape[:3]
    for i in range(rows):
        for k in range(stored):
            row = jnp.clip(col_ref[i, k] - rows, 0, rows - 1)
            out_ref[i, :, k * width : (k + 1) * width] = dot_nt(own_ref[row], a_ref[i, k]).astype(
                BF16
            )


def slot_kernel(slot_ref, far_slot_ref, near_ref, far_ref, out_ref):
    rows, vectors, wide = near_ref.shape
    stored = slot_ref.shape[1]
    width = wide // stored
    for i in range(rows):
        near = near_ref[i].astype(F32)
        far = far_ref[i].astype(F32)
        for p in range(SLOTS):
            total = jnp.zeros((vectors, width), F32)
            for k in range(stored):
                lanes = slice(k * width, (k + 1) * width)
                total = total + jnp.where(slot_ref[i, k] == p, near[:, lanes], 0.0)
                total = total + jnp.where(far_slot_ref[i, k] == p, far[:, lanes], 0.0)
            lanes = slice((p % 2) * width, (p % 2 + 1) * width)
            out_ref[i, p // 2, :, lanes] = total.astype(BF16)


def finish_kernel(where_ref, rest_ref, near_ref, far_ref, scale_ref, out_ref, here_ref):
    rows, _, width = rest_ref.shape
    slot = where_ref[1]
    for i in range(rows):
        scale = scale_ref[i : i + 1, :]
        here = jnp.zeros(rest_ref.shape[1:], F32)
        for h in range(SLOTS // 2):
            total = near_ref[i, h].astype(F32) + far_ref[i, h].astype(F32)
            for q in range(2):
                lanes = slice(q * width, (q + 1) * width)
                value = -scale * total[:, lanes]
                if h == 0 and q == 0:
                    value = rest_ref[i] + value
                out_ref[i, h, :, lanes] = value.astype(BF16)
                here = jnp.where(slot == 2 * h + q, value, here)
        here_ref[i, 0] = here.astype(BF16)


def inverse_factor_kernel(m_ref, out_ref):
    size = m_ref.shape[0]
    rows = [m_ref[v] for v in range(size)]
    place = lax.broadcasted_iota(jnp.int32, rows[0].shape, 0)
    for k in range(size):
        root = lax.rsqrt(rows[k][k : k + 1, :])
        here = place == k
        pivot_row = jnp.where(here, root, rows[k] * root)
        rows[k] = jnp.where(place <= k, pivot_row, 0.0)
        out_ref[k] = rows[k]
        for v in range(k + 1, size):
            rows[v] = jnp.where(here, 0.0, rows[v]) - pivot_row[v : v + 1, :] * pivot_row


def coarse_kernel(
    where_ref, col_ref, place_ref, a_ref, diag_ref, before_ref, own_ref, after_ref, other_ref,
    keep_ref, send_ref, ext, reach, left, total,
):
    rows, stored, width = a_ref.shape[:3]
    vectors = own_ref.shape[2]
    share = rows // 4
    slot = where_ref[1]
    span = reach.shape[1]
    reach[...] = jnp.zeros_like(reach)
    left[...] = jnp.zeros_like(left)

    for s, ref in enumerate((before_ref, own_ref, after_ref)):
        for i in range(rows):
            for h in range(SLOTS // 2):
                block = ref[i, h]
                ext[s * rows + i, 2 * h] = block[:, :width]
                ext[s * rows + i, 2 * h + 1] = block[:, width:]

    def add(i, row, block):
        image = dot_nt(ext[row].reshape(SLOTS * vectors, width), block)
        for q in range(SLOTS):
            at = place_ref[row, q]
            reach[i, at] = reach[i, at] + image[q * vectors : (q + 1) * vectors]

    for i in range(rows):
        for h in range(SLOTS // 2):
            other = other_ref[i, h]
            for q in range(2):
                group = place_ref[rows + i, 2 * h + q] - SLAB_AGGS
                left[i, 0, group] = ext[rows + i, 2 * h + q]
                left[i, 1, group] = other[:, q * width : (q + 1) * width]
        for k in range(stored):
            add(i, col_ref[i, k], a_ref[i, k])

    for r in range(share):
        i = slot * share + r
        add(i, rows + i, diag_ref[i])

    for i in range(rows):
        product = dot_nt(
            reach[i].astype(BF16).reshape(span * vectors, width),
            left[i].reshape(2 * SLAB_AGGS * vectors, width),
        )
        if i == 0:
            total[...] = product
        else:
            total[...] = total[...] + product
    quarter = span * vectors // 4
    for n in range(2):
        start = pl.multiple_of(where_ref[2 + n] * quarter, 32)
        keep_ref[n] = total[pl.ds(start, quarter), :] * (1.0 / width)
        start = pl.multiple_of(where_ref[4 + n] * quarter, 32)
        send_ref[n] = (total[pl.ds(start, quarter), :] * (1.0 / width)).astype(BF16)


def shift(x, by):
    size = lax.axis_size("rows")
    return lax.ppermute(x, "rows", [(i, i + by) for i in range(size) if 0 <= i + by < size])


def partner(slot, core, phase):
    return slot ^ 1 if (core + phase) % 2 == 0 else 3 - slot


def exchange(x, phase):
    pairs = [(2 * s + c, 2 * partner(s, c, phase) + c) for s in range(4) for c in range(2)]
    return lax.ppermute(x, ("aggs", "vecs"), pairs)


def kernel_call(body, name, shapes, operands, scratch=(), limit=12):
    several = isinstance(shapes, list)
    specs = [
        SMEM_SPEC if x.dtype == jnp.int32 else VMEM_SPEC for x in operands
    ]
    return pl.pallas_call(
        body,
        out_shape=shapes,
        in_specs=specs,
        out_specs=[VMEM_SPEC] * len(shapes) if several else VMEM_SPEC,
        scratch_shapes=list(scratch),
        compiler_params=pltpu.CompilerParams(vmem_limit_bytes=limit * 1024 * 1024),
        name=name,
    )(*operands)


def as_block(values, shape):
    padding = [(0, n - m) for n, m in zip(shape, values.shape)]
    return jnp.pad(values, padding).astype(BF16)


def from_block(block, columns):
    return block[:, :columns].astype(F32).astype(jnp.int32)


def on_device(couplings, diag_blocks, coupling_cols, aggregate, pattern, tests):
    rows, vectors, width = tests.shape
    stored = couplings.shape[1]
    half = rows // 2
    slab = lax.axis_index("rows")
    slot = lax.axis_index("aggs")
    core = lax.axis_index("vecs")
    whole_shape = jax.ShapeDtypeStruct((rows, vectors, width), F32)
    extra_shape = (vectors, 2 * width)

    def folded(blocks):
        return jax.ShapeDtypeStruct((blocks, vectors, 2 * width), BF16)

    cols = coupling_cols - slab * rows + rows
    local_aggs = aggregate - slab * SLAB_AGGS
    slot_aggs = jnp.concatenate([aggregate[:, None], pattern], axis=1) - slab * SLAB_AGGS
    inside = cols[:, :, None] == jnp.arange(rows, 2 * rows, dtype=jnp.int32)
    column_aggs = jnp.sum(jnp.where(inside, local_aggs + 1, 0), axis=2) - 1
    hits = column_aggs[:, :, None] == slot_aggs[:, None, :]
    near_slot = jnp.sum(jnp.where(hits, jnp.arange(1, SLOTS + 1, dtype=jnp.int32), 0), axis=2) - 1
    ids_block = as_block(slot_aggs, extra_shape)
    slot_block = as_block(near_slot, extra_shape)
    first = jnp.where(core == 0, slot ^ 1, 3 - slot)
    second = jnp.where(core == 0, 3 - slot, slot ^ 1)
    where = jnp.stack([core, slot, slot, second, first, slot ^ 2]).astype(jnp.int32)

    rounded = kernel_call(fold_kernel, "fold", folded(half), [tests])
    current, scale, places, far_slot = tests, None, None, None
    for sweep in range(SWEEPS):
        before = shift(rounded, 1)
        after = shift(rounded, -1)
        if sweep == 0:
            rest, scale = kernel_call(
                first_center_kernel,
                "first_center",
                [whole_shape, jax.ShapeDtypeStruct((rows, width), F32)],
                [diag_blocks, current],
            )
        else:
            rest = kernel_call(center_kernel, "center", whole_shape, [diag_blocks, current, scale])
        if sweep == 1:
            places = jnp.concatenate(
                [
                    from_block(before[half], SLOTS),
                    slot_aggs + SLAB_AGGS,
                    from_block(after[half], SLOTS) + 2 * SLAB_AGGS,
                ],
                axis=0,
            )
        last = sweep == SWEEPS - 1
        part = kernel_call(
            couple_kernel,
            "couple",
            folded(half + last),
            [cols, couplings, before, rounded, after] + [slot_block] * last,
            [pltpu.VMEM((3 * rows, vectors, width), BF16)],
        )
        far = exchange(part, 0)
        if last:
            far_slot = from_block(far[half], stored)
            part, far = part[:half], far[:half]
        pair = (part.astype(F32) + far.astype(F32)).astype(BF16)
        far = exchange(pair, 1)
        current, rounded = kernel_call(
            update_kernel,
            "update",
            [whole_shape, folded(half + (sweep == 0))],
            [rest, pair, far, scale] + [ids_block] * (sweep == 0),
        )

    every = lax.all_gather(current, "vecs", axis=1, tiled=True)
    grams = jnp.einsum("ivb,iwb->ivw", every, every, precision=HIGHEST_PRECISION)
    members = (local_aggs[:, None] == jnp.arange(SLAB_AGGS, dtype=jnp.int32)[None, :]).astype(F32)
    totals = jnp.einsum("ig,ivw->vwg", members, grams, precision=HIGHEST_PRECISION) / width
    inverse = kernel_call(
        inverse_factor_kernel,
        "inverse_factor",
        jax.ShapeDtypeStruct((VECTORS, VECTORS, SLAB_AGGS), F32),
        [totals],
    )
    own_inverse = lax.dynamic_slice_in_dim(inverse, core * vectors, vectors, 0)
    row_inverse = jnp.einsum("ig,cvg->icv", members, own_inverse, precision=HIGHEST_PRECISION)
    tentative = jnp.einsum("icv,ivb->icb", row_inverse, every, precision=HIGHEST_PRECISION)

    moved = kernel_call(
        fit_kernel, "fit", folded(rows), [cols, couplings, tentative.astype(BF16)]
    )
    rest = kernel_call(center_kernel, "center", whole_shape, [diag_blocks, tentative, scale])
    slots_shape = jax.ShapeDtypeStruct((rows, SLOTS // 2, vectors, 2 * width), BF16)
    pair = kernel_call(
        slot_kernel, "slots", slots_shape, [near_slot, far_slot, moved, exchange(moved, 0)]
    )
    prolong, prolong_here = kernel_call(
        finish_kernel,
        "finish",
        [slots_shape, jax.ShapeDtypeStruct((rows, 1, vectors, width), BF16)],
        [where, rest, pair, exchange(pair, 1), scale],
    )

    before = shift(prolong, 1)
    after = shift(prolong, -1)
    other = lax.ppermute(prolong, "vecs", [(0, 1), (1, 0)])
    span = 3 * SLAB_AGGS
    quarter = span * vectors // 4
    wide = SLAB_AGGS * 2 * vectors
    keep, send = kernel_call(
        coarse_kernel,
        "coarse",
        [
            jax.ShapeDtypeStruct((2, quarter, wide), F32),
            jax.ShapeDtypeStruct((2, quarter, wide), BF16),
        ],
        [where, cols, places, couplings, diag_blocks, before, prolong, after, other],
        [
            pltpu.VMEM((3 * rows, SLOTS, vectors, width), BF16),
            pltpu.VMEM((rows, span, vectors, width), F32),
            pltpu.VMEM((rows, 2, SLAB_AGGS, vectors, width), BF16),
            pltpu.VMEM((span * vectors, wide), F32),
        ],
        limit=28,
    )
    merged = keep + exchange(send, 0).astype(F32)
    owned = merged[0] + exchange(merged[1].astype(BF16), 1).astype(F32)
    mine, theirs = owned[:, : wide // 2], owned[:, wide // 2 :]
    theirs = lax.ppermute(theirs, "vecs", [(0, 1), (1, 0)])
    low = jnp.where(core == 0, mine, theirs).reshape(span // 4, vectors, -1)
    high = jnp.where(core == 0, theirs, mine).reshape(span // 4, vectors, -1)
    coarse = jnp.concatenate([low, high], axis=1).reshape(span // 4, VECTORS, SLAB_AGGS, vectors)
    return (prolong_here, coarse.transpose(2, 0, 3, 1))


def solution(mesh):
    return jax.shard_map(
        on_device,
        mesh=mesh,
        in_specs=(
            P("rows", "aggs", None, None),
            P("rows", None, None),
            P("rows", "aggs"),
            P("rows"),
            P("rows", None),
            P("rows", "vecs", None),
        ),
        out_specs=(P("rows", "aggs", "vecs", None), P("rows", "aggs", "vecs", None)),
        check_vma=False,
    )
```

```python
import jax
import jax.numpy as jnp
from jax import lax
from jax.experimental import pallas as pl
from jax.experimental.pallas import tpu as pltpu
from jax.sharding import PartitionSpec as P

VECTORS = 32
SWEEPS = 3
SLAB_AGGS = 8
SLOTS = 4
DAMPING = 2.0 / 3.0
HIGHEST_PRECISION = lax.Precision.HIGHEST
BF16 = jnp.bfloat16
F32 = jnp.float32

SMEM_SPEC = pl.BlockSpec(memory_space=pltpu.SMEM)
VMEM_SPEC = pl.BlockSpec(memory_space=pltpu.VMEM)


def dot_nt(left, right):
    return lax.dot_general(left, right, (((1,), (1,)), ((), ())), preferred_element_type=F32)


LANES = 128


def put(ref, low, high):
    width = low.shape[-1]
    ref[:, :width] = low.astype(ref.dtype)
    ref[:, width : 2 * width - LANES] = high[:, LANES:].astype(ref.dtype)
    ref[:, 2 * width - LANES :] = high[:, :LANES].astype(ref.dtype)


def take_into(low_ref, high_ref, block):
    width = block.shape[-1] // 2
    low_ref[...] = block[:, :width]
    high_ref[:, :LANES] = block[:, 2 * width - LANES :]
    high_ref[:, LANES:] = block[:, width : 2 * width - LANES]


def center_kernel(diag_ref, x_ref, scale_ref, y_ref):
    half = x_ref.shape[0] // 2

    def rest(i):
        x = x_ref[i]
        return x - scale_ref[i : i + 1, :] * dot_nt(x.astype(BF16), diag_ref[i])

    for m in range(half):
        put(y_ref.at[m], rest(m), rest(half + m))


def folded_center_kernel(diag_ref, x_ref, scale_ref, y_ref, rows):
    half = x_ref.shape[0]
    for m in range(half):
        take_into(rows.at[m], rows.at[half + m], x_ref[m])
    center_kernel(diag_ref, rows, scale_ref, y_ref)


def first_center_kernel(diag_ref, x_ref, y_ref, scale_ref, folded_scale_ref):
    rows, _, width = x_ref.shape
    on_diagonal = lax.broadcasted_iota(jnp.int32, (width, width), 0) == lax.broadcasted_iota(
        jnp.int32, (width, width), 1
    )
    for i in range(rows):
        block = diag_ref[i].astype(F32)
        pivot = jnp.sum(jnp.where(on_diagonal, block, 0.0), axis=0, keepdims=True)
        scale_ref[i : i + 1, :] = DAMPING / pivot
    for m in range(rows // 2):
        put(
            folded_scale_ref.at[m : m + 1],
            scale_ref[m : m + 1, :],
            scale_ref[rows // 2 + m : rows // 2 + m + 1, :],
        )
    center_kernel(diag_ref, x_ref, scale_ref, y_ref)


def fold_kernel(x_ref, out_ref):
    half = out_ref.shape[0]
    for m in range(half):
        put(out_ref.at[m], x_ref[m], x_ref[half + m])


def stage_kernel(a_ref, diag_ref, a_out_ref, diag_out_ref, sems):
    copies = [
        pltpu.make_async_copy(a_ref, a_out_ref, sems.at[0]),
        pltpu.make_async_copy(diag_ref, diag_out_ref, sems.at[1]),
    ]
    for copy in copies:
        copy.start()
    for copy in copies:
        copy.wait()


def pair_kernel(near_ref, far_ref, out_ref):
    for m in range(out_ref.shape[0]):
        out_ref[m] = (near_ref[m].astype(F32) + far_ref[m].astype(F32)).astype(BF16)


def updated(m, rest_ref, near_ref, far_ref, scale_ref):
    total = near_ref[m].astype(F32) + far_ref[m].astype(F32)
    return rest_ref[m] - scale_ref[m : m + 1, :] * total


def update_kernel(rest_ref, near_ref, far_ref, scale_ref, *refs):
    half = rest_ref.shape[0]
    extra_ref = refs[0] if len(refs) == 3 else None
    x_ref, rounded_ref = refs[-2:]
    for m in range(half):
        x = updated(m, rest_ref, near_ref, far_ref, scale_ref)
        x_ref[m] = x
        rounded_ref[m] = x.astype(BF16)
    if extra_ref is not None:
        rounded_ref[half] = extra_ref[...]


def last_update_kernel(rest_ref, near_ref, far_ref, scale_ref, x_ref):
    half = rest_ref.shape[0]
    for m in range(half):
        x = updated(m, rest_ref, near_ref, far_ref, scale_ref)
        take_into(x_ref.at[m], x_ref.at[half + m], x)


def couple_kernel(col_ref, a_ref, before_ref, own_ref, after_ref, *refs):
    rows, stored = a_ref.shape[:2]
    half = rows // 2
    extra_ref = refs[0] if len(refs) == 3 else None
    out_ref, ext = refs[-2:]
    for s, ref in enumerate((before_ref, own_ref, after_ref)):
        for m in range(half):
            take_into(ext.at[s * rows + m], ext.at[s * rows + half + m], ref[m])

    def product(i):
        total = dot_nt(ext[col_ref[i, 0]], a_ref[i, 0])
        for k in range(1, stored):
            total = total + dot_nt(ext[col_ref[i, k]], a_ref[i, k])
        return total

    for m in range(half):
        put(out_ref.at[m], product(m), product(half + m))
    if extra_ref is not None:
        out_ref[half] = extra_ref[...]


def fit_kernel(col_ref, a_ref, own_ref, out_ref):
    rows, stored = a_ref.shape[:2]
    half = rows // 2

    def product(i, k):
        row = jnp.clip(col_ref[i, k] - rows, 0, rows - 1)
        return dot_nt(own_ref[row], a_ref[i, k])

    for m in range(half):
        for k in range(stored):
            put(out_ref.at[m, k], product(m, k), product(half + m, k))


def slot_kernel(slot_ref, far_slot_ref, near_ref, far_ref, out_ref):
    half, stored, vectors, wide = near_ref.shape
    is_low = lax.broadcasted_iota(jnp.int32, (vectors, wide), 1) < wide // 2
    for m in range(half):
        terms = []
        for ids_ref, ref in ((slot_ref, near_ref), (far_slot_ref, far_ref)):
            for k in range(stored):
                ids = jnp.where(is_low, ids_ref[m, k], ids_ref[half + m, k])
                terms.append((ids, ref[m, k].astype(F32)))
        for p in range(SLOTS):
            total = jnp.zeros((vectors, wide), F32)
            for ids, value in terms:
                total = total + jnp.where(ids == p, value, 0.0)
            out_ref[m, p] = total.astype(BF16)


def finish_kernel(where_ref, rest_ref, near_ref, far_ref, scale_ref, out_ref, here_ref):
    half = rest_ref.shape[0]
    slot = where_ref[1]
    for m in range(half):
        scale = scale_ref[m : m + 1, :]
        here = jnp.zeros(rest_ref.shape[1:], F32)
        for p in range(SLOTS):
            total = near_ref[m, p].astype(F32) + far_ref[m, p].astype(F32)
            value = -scale * total
            if p == 0:
                value = rest_ref[m] + value
            out_ref[m, p] = value.astype(BF16)
            here = jnp.where(slot == p, value, here)
        take_into(here_ref.at[m, 0], here_ref.at[half + m, 0], here.astype(BF16))


def inverse_factor_kernel(m_ref, out_ref):
    size = m_ref.shape[0]
    rows = [m_ref[v] for v in range(size)]
    place = lax.broadcasted_iota(jnp.int32, rows[0].shape, 0)
    for k in range(size):
        root = lax.rsqrt(rows[k][k : k + 1, :])
        here = place == k
        pivot_row = jnp.where(here, root, rows[k] * root)
        rows[k] = jnp.where(place <= k, pivot_row, 0.0)
        out_ref[k] = rows[k]
        for v in range(k + 1, size):
            rows[v] = jnp.where(here, 0.0, rows[v]) - pivot_row[v : v + 1, :] * pivot_row


def coarse_kernel(
    where_ref, col_ref, place_ref, a_ref, diag_ref, before_ref, own_ref, after_ref, other_ref,
    keep_ref, send_ref, ext, reach, left, total,
):
    rows, stored, width = a_ref.shape[:3]
    vectors = own_ref.shape[2]
    share = rows // 4
    slot = where_ref[1]
    span = reach.shape[1]
    reach[...] = jnp.zeros_like(reach)
    left[...] = jnp.zeros_like(left)

    half = rows // 2
    for s, ref in enumerate((before_ref, own_ref, after_ref)):
        for m in range(half):
            for p in range(SLOTS):
                low, high = s * rows + m, s * rows + half + m
                take_into(ext.at[low, p], ext.at[high, p], ref[m, p])

    def add(i, row, block):
        image = dot_nt(ext[row].reshape(SLOTS * vectors, width), block)
        for q in range(SLOTS):
            at = place_ref[row, q]
            reach[i, at] = reach[i, at] + image[q * vectors : (q + 1) * vectors]

    for m in range(half):
        for p in range(SLOTS):
            low = place_ref[rows + m, p] - SLAB_AGGS
            high = place_ref[rows + half + m, p] - SLAB_AGGS
            left[m, 0, low] = ext[rows + m, p]
            left[half + m, 0, high] = ext[rows + half + m, p]
            take_into(left.at[m, 1, low], left.at[half + m, 1, high], other_ref[m, p])
    for i in range(rows):
        for k in range(stored):
            add(i, col_ref[i, k], a_ref[i, k])

    for r in range(share):
        i = slot * share + r
        add(i, rows + i, diag_ref[i])

    for i in range(rows):
        product = dot_nt(
            reach[i].astype(BF16).reshape(span * vectors, width),
            left[i].reshape(2 * SLAB_AGGS * vectors, width),
        )
        if i == 0:
            total[...] = product
        else:
            total[...] = total[...] + product
    quarter = span * vectors // 4
    for n in range(2):
        start = pl.multiple_of(where_ref[2 + n] * quarter, 32)
        keep_ref[n] = total[pl.ds(start, quarter), :] * (1.0 / width)
        start = pl.multiple_of(where_ref[4 + n] * quarter, 32)
        send_ref[n] = (total[pl.ds(start, quarter), :] * (1.0 / width)).astype(BF16)


def shift(x, by):
    size = lax.axis_size("rows")
    return lax.ppermute(x, "rows", [(i, i + by) for i in range(size) if 0 <= i + by < size])


def partner(slot, core, phase):
    return slot ^ 1 if (core + phase) % 2 == 0 else 3 - slot


def exchange(x, phase):
    pairs = [(2 * s + c, 2 * partner(s, c, phase) + c) for s in range(4) for c in range(2)]
    return lax.ppermute(x, ("aggs", "vecs"), pairs)


def kernel_call(body, name, shapes, operands, scratch=(), limit=12):
    several = isinstance(shapes, list)
    specs = [
        SMEM_SPEC if x.dtype == jnp.int32 else VMEM_SPEC for x in operands
    ]
    return pl.pallas_call(
        body,
        out_shape=shapes,
        in_specs=specs,
        out_specs=[VMEM_SPEC] * len(shapes) if several else VMEM_SPEC,
        scratch_shapes=list(scratch),
        compiler_params=pltpu.CompilerParams(vmem_limit_bytes=limit * 1024 * 1024),
        name=name,
    )(*operands)


def as_block(values, shape):
    padding = [(0, n - m) for n, m in zip(shape, values.shape)]
    return jnp.pad(values, padding).astype(BF16)


def from_block(block, columns):
    return block[:, :columns].astype(F32).astype(jnp.int32)


def on_device(couplings, diag_blocks, coupling_cols, aggregate, pattern, tests):
    rows, vectors, width = tests.shape
    stored = couplings.shape[1]
    half = rows // 2
    slab = lax.axis_index("rows")
    slot = lax.axis_index("aggs")
    core = lax.axis_index("vecs")
    whole_shape = jax.ShapeDtypeStruct((rows, vectors, width), F32)
    extra_shape = (vectors, 2 * width)

    def folded(blocks):
        return jax.ShapeDtypeStruct((blocks, vectors, 2 * width), BF16)

    cols = coupling_cols - slab * rows + rows
    local_aggs = aggregate - slab * SLAB_AGGS
    slot_aggs = jnp.concatenate([aggregate[:, None], pattern], axis=1) - slab * SLAB_AGGS
    inside = cols[:, :, None] == jnp.arange(rows, 2 * rows, dtype=jnp.int32)
    column_aggs = jnp.sum(jnp.where(inside, local_aggs + 1, 0), axis=2) - 1
    hits = column_aggs[:, :, None] == slot_aggs[:, None, :]
    near_slot = jnp.sum(jnp.where(hits, jnp.arange(1, SLOTS + 1, dtype=jnp.int32), 0), axis=2) - 1
    ids_block = as_block(slot_aggs, extra_shape)
    slot_block = as_block(near_slot, extra_shape)
    first = jnp.where(core == 0, slot ^ 1, 3 - slot)
    second = jnp.where(core == 0, 3 - slot, slot ^ 1)
    where = jnp.stack([core, slot, slot, second, first, slot ^ 2]).astype(jnp.int32)

    folded_whole = jax.ShapeDtypeStruct((half, vectors, 2 * width), F32)
    couplings, diag_blocks = pl.pallas_call(
        stage_kernel,
        out_shape=[pltpu.VMEM(x.shape, x.dtype) for x in (couplings, diag_blocks)],
        in_specs=[pl.BlockSpec(memory_space=pl.ANY)] * 2,
        out_specs=[VMEM_SPEC] * 2,
        scratch_shapes=[pltpu.SemaphoreType.DMA((2,))],
        compiler_params=pltpu.CompilerParams(vmem_limit_bytes=8 * 1024 * 1024),
        cost_estimate=pl.CostEstimate(flops=0, bytes_accessed=16000000, transcendentals=0),
        name="stage",
    )(couplings, diag_blocks)
    rounded = kernel_call(fold_kernel, "fold", folded(half), [tests])
    current, scale, folded_scale, places, far_slot = tests, None, None, None, None
    for sweep in range(SWEEPS):
        last = sweep == SWEEPS - 1
        before = shift(rounded, 1)
        after = shift(rounded, -1)
        if sweep == 0:
            rest, scale, folded_scale = kernel_call(
                first_center_kernel,
                "first_center",
                [
                    folded_whole,
                    jax.ShapeDtypeStruct((rows, width), F32),
                    jax.ShapeDtypeStruct((half, 2 * width), F32),
                ],
                [diag_blocks, current],
            )
        else:
            rest = kernel_call(
                folded_center_kernel,
                "center",
                folded_whole,
                [diag_blocks, current, scale],
                [pltpu.VMEM((rows, vectors, width), F32)],
            )
        if sweep == 1:
            places = jnp.concatenate(
                [
                    from_block(before[half], SLOTS),
                    slot_aggs + SLAB_AGGS,
                    from_block(after[half], SLOTS) + 2 * SLAB_AGGS,
                ],
                axis=0,
            )
        part = kernel_call(
            couple_kernel,
            "couple",
            folded(half + last),
            [cols, couplings, before, rounded, after] + [slot_block] * last,
            [pltpu.VMEM((3 * rows, vectors, width), BF16)],
        )
        far = exchange(part, 0)
        if last:
            far_slot = from_block(far[half], stored)
        pair = kernel_call(pair_kernel, "pair", folded(half), [part, far])
        operands = [rest, pair, exchange(pair, 1), folded_scale]
        if last:
            current = kernel_call(last_update_kernel, "last_update", whole_shape, operands)
        else:
            current, rounded = kernel_call(
                update_kernel,
                "update",
                [folded_whole, folded(half + (sweep == 0))],
                operands + [ids_block] * (sweep == 0),
            )

    every = lax.all_gather(current, "vecs", axis=1, tiled=True)
    grams = jnp.einsum("ivb,iwb->ivw", every, every, precision=HIGHEST_PRECISION)
    members = (local_aggs[:, None] == jnp.arange(SLAB_AGGS, dtype=jnp.int32)[None, :]).astype(F32)
    totals = jnp.einsum("ig,ivw->vwg", members, grams, precision=HIGHEST_PRECISION) / width
    inverse = kernel_call(
        inverse_factor_kernel,
        "inverse_factor",
        jax.ShapeDtypeStruct((VECTORS, VECTORS, SLAB_AGGS), F32),
        [totals],
    )
    own_inverse = lax.dynamic_slice_in_dim(inverse, core * vectors, vectors, 0)
    row_inverse = jnp.einsum("ig,cvg->icv", members, own_inverse, precision=HIGHEST_PRECISION)
    tentative = jnp.einsum("icv,ivb->icb", row_inverse, every, precision=HIGHEST_PRECISION)

    moved = kernel_call(
        fit_kernel,
        "fit",
        jax.ShapeDtypeStruct((half, stored, vectors, 2 * width), BF16),
        [cols, couplings, tentative.astype(BF16)]
    )
    rest = kernel_call(center_kernel, "center", folded_whole, [diag_blocks, tentative, scale])
    slots_shape = jax.ShapeDtypeStruct((half, SLOTS, vectors, 2 * width), BF16)
    pair = kernel_call(
        slot_kernel, "slots", slots_shape, [near_slot, far_slot, moved, exchange(moved, 0)]
    )
    prolong, prolong_here = kernel_call(
        finish_kernel,
        "finish",
        [slots_shape, jax.ShapeDtypeStruct((rows, 1, vectors, width), BF16)],
        [where, rest, pair, exchange(pair, 1), folded_scale],
    )

    before = shift(prolong, 1)
    after = shift(prolong, -1)
    other = lax.ppermute(prolong, "vecs", [(0, 1), (1, 0)])
    span = 3 * SLAB_AGGS
    quarter = span * vectors // 4
    wide = SLAB_AGGS * 2 * vectors
    keep, send = kernel_call(
        coarse_kernel,
        "coarse",
        [
            jax.ShapeDtypeStruct((2, quarter, wide), F32),
            jax.ShapeDtypeStruct((2, quarter, wide), BF16),
        ],
        [where, cols, places, couplings, diag_blocks, before, prolong, after, other],
        [
            pltpu.VMEM((3 * rows, SLOTS, vectors, width), BF16),
            pltpu.VMEM((rows, span, vectors, width), F32),
            pltpu.VMEM((rows, 2, SLAB_AGGS, vectors, width), BF16),
            pltpu.VMEM((span * vectors, wide), F32),
        ],
        limit=28,
    )
    merged = keep + exchange(send, 0).astype(F32)
    owned = merged[0] + exchange(merged[1].astype(BF16), 1).astype(F32)
    mine, theirs = owned[:, : wide // 2], owned[:, wide // 2 :]
    theirs = lax.ppermute(theirs, "vecs", [(0, 1), (1, 0)])
    low = jnp.where(core == 0, mine, theirs).reshape(span // 4, vectors, -1)
    high = jnp.where(core == 0, theirs, mine).reshape(span // 4, vectors, -1)
    coarse = jnp.concatenate([low, high], axis=1).reshape(span // 4, VECTORS, SLAB_AGGS, vectors)
    return (prolong_here, coarse.transpose(2, 0, 3, 1))


def solution(mesh):
    return jax.shard_map(
        on_device,
        mesh=mesh,
        in_specs=(
            P("rows", "aggs", None, None),
            P("rows", None, None),
            P("rows", "aggs"),
            P("rows"),
            P("rows", None),
            P("rows", "vecs", None),
        ),
        out_specs=(P("rows", "aggs", "vecs", None), P("rows", "aggs", "vecs", None)),
        check_vma=False,
    )
```

```python
import jax
import jax.numpy as jnp
from jax import lax
from jax.experimental import pallas as pl
from jax.experimental.pallas import tpu as pltpu
from jax.sharding import PartitionSpec as P

VECTORS = 32
SWEEPS = 3
SLAB_AGGS = 8
SLOTS = 4
DAMPING = 2.0 / 3.0
HIGHEST_PRECISION = lax.Precision.HIGHEST
BF16 = jnp.bfloat16
F32 = jnp.float32

SMEM_SPEC = pl.BlockSpec(memory_space=pltpu.SMEM)
VMEM_SPEC = pl.BlockSpec(memory_space=pltpu.VMEM)
HBM_SPEC = pl.BlockSpec(memory_space=pltpu.HBM)


def dot_nt(left, right):
    return lax.dot_general(left, right, (((1,), (1,)), ((), ())), preferred_element_type=F32)


LANES = 128


def put(ref, low, high):
    width = low.shape[-1]
    ref[:, :width] = low.astype(ref.dtype)
    ref[:, width : 2 * width - LANES] = high[:, LANES:].astype(ref.dtype)
    ref[:, 2 * width - LANES :] = high[:, :LANES].astype(ref.dtype)


def take_into(low_ref, high_ref, block):
    width = block.shape[-1] // 2
    low_ref[...] = block[:, :width]
    high_ref[:, :LANES] = block[:, 2 * width - LANES :]
    high_ref[:, LANES:] = block[:, width : 2 * width - LANES]


CHUNK = 2


def fetches(source_ref, held_ref, sems):
    half = source_ref.shape[0] // 2
    copies = []
    for c in range(half // CHUNK):
        for start in (c * CHUNK, half + c * CHUNK):
            rows = pl.ds(start, CHUNK)
            copies.append(
                pltpu.make_async_copy(
                    source_ref.at[rows], held_ref.at[rows], sems.at[len(copies)]
                )
            )
    for copy in copies:
        copy.start()

    def ready(m):
        if m % CHUNK == 0:
            for copy in copies[2 * (m // CHUNK) : 2 * (m // CHUNK) + 2]:
                copy.wait()

    return ready


def center_kernel(source_ref, x_ref, scale_ref, y_ref, diag_ref, sems, ready=None):
    half = x_ref.shape[0] // 2
    if ready is None:
        ready = fetches(source_ref, diag_ref, sems)

    def rest(i):
        x = x_ref[i]
        return x - scale_ref[i : i + 1, :] * dot_nt(x.astype(BF16), diag_ref[i])

    for m in range(half):
        ready(m)
        put(y_ref.at[m], rest(m), rest(half + m))


def folded_center_kernel(source_ref, x_ref, scale_ref, y_ref, diag_ref, sems, rows):
    half = x_ref.shape[0]
    ready = fetches(source_ref, diag_ref, sems)
    for m in range(half):
        take_into(rows.at[m], rows.at[half + m], x_ref[m])
    center_kernel(source_ref, rows, scale_ref, y_ref, diag_ref, sems, ready)


def first_center_kernel(source_ref, x_ref, y_ref, scale_ref, folded_scale_ref, diag_ref, sems):
    rows, _, width = x_ref.shape
    copy = pltpu.make_async_copy(source_ref, diag_ref, sems.at[0])
    copy.start()
    copy.wait()
    on_diagonal = lax.broadcasted_iota(jnp.int32, (width, width), 0) == lax.broadcasted_iota(
        jnp.int32, (width, width), 1
    )
    for i in range(rows):
        block = diag_ref[i].astype(F32)
        pivot = jnp.sum(jnp.where(on_diagonal, block, 0.0), axis=0, keepdims=True)
        scale_ref[i : i + 1, :] = DAMPING / pivot
    for m in range(rows // 2):
        put(
            folded_scale_ref.at[m : m + 1],
            scale_ref[m : m + 1, :],
            scale_ref[rows // 2 + m : rows // 2 + m + 1, :],
        )
    center_kernel(source_ref, x_ref, scale_ref, y_ref, diag_ref, sems, lambda m: None)


def fold_kernel(x_ref, out_ref):
    half = out_ref.shape[0]
    for m in range(half):
        put(out_ref.at[m], x_ref[m], x_ref[half + m])


def stage_kernel(source_ref, out_ref, a_ref, sems):
    half = source_ref.shape[0] // 2
    ready = fetches(source_ref, a_ref, sems)
    for m in range(half):
        ready(m)
        for i in (m, half + m):
            put(out_ref.at[i], a_ref[i, 0], a_ref[i, 1])


def spread(low_ref, high_ref, main, rest):
    zero = jnp.zeros_like(rest)
    low_ref[:, :LANES] = main
    low_ref[:, LANES:] = jnp.concatenate([rest, zero], axis=1)
    high_ref[:, LANES:] = main
    high_ref[:, :LANES] = jnp.concatenate([zero, rest], axis=1)


def spread_folded(low_ref, high_ref, first, second, block):
    wide = block.shape[-1]
    width = wide // 2
    spread(low_ref.at[first], high_ref.at[first], block[:, :LANES], block[:, LANES:width])
    spread(
        low_ref.at[second],
        high_ref.at[second],
        block[:, wide - LANES :],
        block[:, width : wide - LANES],
    )


def joined(low, high):
    return jnp.concatenate(
        [low[:, :LANES], low[:, LANES:] + high[:, :LANES], high[:, LANES:]], axis=1
    )


def stacked(low, high):
    zero = jnp.zeros((low.shape[0], LANES), low.dtype)
    return jnp.concatenate(
        [jnp.concatenate([low, zero], axis=1), jnp.concatenate([zero, high], axis=1)], axis=0
    )


def pair_kernel(near_ref, far_ref, out_ref):
    for m in range(out_ref.shape[0]):
        out_ref[m] = (near_ref[m].astype(F32) + far_ref[m].astype(F32)).astype(BF16)


def updated(m, rest_ref, near_ref, far_ref, scale_ref):
    total = near_ref[m].astype(F32) + far_ref[m].astype(F32)
    return rest_ref[m] - scale_ref[m : m + 1, :] * total


def update_kernel(rest_ref, near_ref, far_ref, scale_ref, *refs):
    half = rest_ref.shape[0]
    extra_ref = refs[0] if len(refs) == 3 else None
    x_ref, rounded_ref = refs[-2:]
    for m in range(half):
        x = updated(m, rest_ref, near_ref, far_ref, scale_ref)
        x_ref[m] = x
        rounded_ref[m] = x.astype(BF16)
    if extra_ref is not None:
        rounded_ref[half] = extra_ref[...]


def last_update_kernel(rest_ref, near_ref, far_ref, scale_ref, x_ref):
    half = rest_ref.shape[0]
    for m in range(half):
        x = updated(m, rest_ref, near_ref, far_ref, scale_ref)
        take_into(x_ref.at[m], x_ref.at[half + m], x)


def couple_kernel(col_ref, a_ref, before_ref, own_ref, after_ref, *refs):
    rows = a_ref.shape[0]
    half = rows // 2
    extra_ref = refs[0] if len(refs) == 4 else None
    out_ref, low, high = refs[-3:]
    for s, ref in enumerate((before_ref, own_ref, after_ref)):
        for m in range(half):
            spread_folded(low, high, s * rows + m, s * rows + half + m, ref[m])

    def product(i):
        return dot_nt(joined(low[col_ref[i, 0]], high[col_ref[i, 1]]), a_ref[i])

    for m in range(half):
        put(out_ref.at[m], product(m), product(half + m))
    if extra_ref is not None:
        out_ref[half] = extra_ref[...]


def fit_kernel(col_ref, a_ref, own_ref, out_ref, low, high):
    rows, vectors, width = own_ref.shape
    half = rows // 2
    for i in range(rows):
        own = own_ref[i]
        spread(low.at[i], high.at[i], own[:, :LANES], own[:, LANES:])

    def products(i):
        first, second = (jnp.clip(col_ref[i, k] - rows, 0, rows - 1) for k in range(2))
        return dot_nt(stacked(low[first], high[second]), a_ref[i])

    for m in range(half):
        near, far = products(m), products(half + m)
        for k in range(2):
            part = slice(k * vectors, (k + 1) * vectors)
            put(out_ref.at[m, k], near[part], far[part])


def slot_kernel(slot_ref, far_slot_ref, near_ref, far_ref, out_ref):
    half, stored, vectors, wide = near_ref.shape
    is_low = lax.broadcasted_iota(jnp.int32, (vectors, wide), 1) < wide // 2
    for m in range(half):
        terms = []
        for ids_ref, ref in ((slot_ref, near_ref), (far_slot_ref, far_ref)):
            for k in range(stored):
                ids = jnp.where(is_low, ids_ref[m, k], ids_ref[half + m, k])
                terms.append((ids, ref[m, k].astype(F32)))
        for p in range(SLOTS):
            total = jnp.zeros((vectors, wide), F32)
            for ids, value in terms:
                total = total + jnp.where(ids == p, value, 0.0)
            out_ref[m, p] = total.astype(BF16)


def finish_kernel(where_ref, rest_ref, near_ref, far_ref, scale_ref, out_ref, here_ref):
    half = rest_ref.shape[0]
    slot = where_ref[1]
    for m in range(half):
        scale = scale_ref[m : m + 1, :]
        here = jnp.zeros(rest_ref.shape[1:], F32)
        for p in range(SLOTS):
            total = near_ref[m, p].astype(F32) + far_ref[m, p].astype(F32)
            value = -scale * total
            if p == 0:
                value = rest_ref[m] + value
            out_ref[m, p] = value.astype(BF16)
            here = jnp.where(slot == p, value, here)
        take_into(here_ref.at[m, 0], here_ref.at[half + m, 0], here.astype(BF16))


def inverse_factor_kernel(m_ref, out_ref):
    size = m_ref.shape[0]
    rows = [m_ref[v] for v in range(size)]
    place = lax.broadcasted_iota(jnp.int32, rows[0].shape, 0)
    for k in range(size):
        root = lax.rsqrt(rows[k][k : k + 1, :])
        here = place == k
        pivot_row = jnp.where(here, root, rows[k] * root)
        rows[k] = jnp.where(place <= k, pivot_row, 0.0)
        out_ref[k] = rows[k]
        for v in range(k + 1, size):
            rows[v] = jnp.where(here, 0.0, rows[v]) - pivot_row[v : v + 1, :] * pivot_row


def coarse_kernel(
    where_ref, col_ref, place_ref, a_ref, diag_source_ref, before_ref, own_ref, after_ref, other_ref,
    keep_ref, send_ref, low, high, reach, left, total, diag_ref, diag_sem,
):
    rows, width = a_ref.shape[:2]
    vectors = own_ref.shape[2]
    share = rows // 4
    slot = where_ref[1]
    span = reach.shape[1]
    diag_copy = pltpu.make_async_copy(
        diag_source_ref.at[pl.ds(slot * share, share)], diag_ref, diag_sem.at[0]
    )
    diag_copy.start()
    reach[...] = jnp.zeros_like(reach)
    left[...] = jnp.zeros_like(left)

    half = rows // 2
    for s, ref in enumerate((before_ref, own_ref, after_ref)):
        for m in range(half):
            for p in range(SLOTS):
                spread_folded(
                    low.at[:, p], high.at[:, p], s * rows + m, s * rows + half + m, ref[m, p]
                )

    span_rows = SLOTS * vectors

    def add(i, row, image):
        for q in range(SLOTS):
            at = place_ref[row, q]
            reach[i, at] = reach[i, at] + image[q * vectors : (q + 1) * vectors]

    for m in range(half):
        for p in range(SLOTS):
            first = place_ref[rows + m, p] - SLAB_AGGS
            second = place_ref[rows + half + m, p] - SLAB_AGGS
            for side, ref in enumerate((own_ref, other_ref)):
                take_into(left.at[m, side, first], left.at[half + m, side, second], ref[m, p])
    for m in range(half):
        for i in (m, half + m):
            first, second = col_ref[i, 0], col_ref[i, 1]
            images = dot_nt(
                stacked(
                    low[first].reshape(span_rows, 2 * LANES),
                    high[second].reshape(span_rows, 2 * LANES),
                ),
                a_ref[i],
            )
            add(i, first, images[:span_rows])
            add(i, second, images[span_rows:])

    diag_copy.wait()
    for r in range(share):
        i = slot * share + r
        own = low[rows + i].reshape(span_rows, 2 * LANES)[:, :width]
        add(i, rows + i, dot_nt(own, diag_ref[r]))

    for i in range(rows):
        product = dot_nt(
            reach[i].astype(BF16).reshape(span * vectors, width),
            left[i].reshape(2 * SLAB_AGGS * vectors, width),
        )
        if i == 0:
            total[...] = product
        else:
            total[...] = total[...] + product
    quarter = span * vectors // 4
    for n in range(2):
        start = pl.multiple_of(where_ref[2 + n] * quarter, 32)
        keep_ref[n] = total[pl.ds(start, quarter), :] * (1.0 / width)
        start = pl.multiple_of(where_ref[4 + n] * quarter, 32)
        send_ref[n] = (total[pl.ds(start, quarter), :] * (1.0 / width)).astype(BF16)


def shift(x, by):
    size = lax.axis_size("rows")
    return lax.ppermute(x, "rows", [(i, i + by) for i in range(size) if 0 <= i + by < size])


def partner(slot, core, phase):
    return slot ^ 1 if (core + phase) % 2 == 0 else 3 - slot


def exchange(x, phase):
    pairs = [(2 * s + c, 2 * partner(s, c, phase) + c) for s in range(4) for c in range(2)]
    return lax.ppermute(x, ("aggs", "vecs"), pairs)


def kernel_call(body, name, shapes, operands, scratch=(), limit=12):
    several = isinstance(shapes, list)
    is_block = [x.ndim == 3 and x.shape[-1] == x.shape[-2] and x.dtype == BF16 for x in operands]
    specs = [
        SMEM_SPEC if x.dtype == jnp.int32 else HBM_SPEC if block else VMEM_SPEC
        for x, block in zip(operands, is_block)
    ]
    operands = [
        pltpu.with_memory_space_constraint(x, pltpu.HBM) if block else x
        for x, block in zip(operands, is_block)
    ]
    return pl.pallas_call(
        body,
        out_shape=shapes,
        in_specs=specs,
        out_specs=[VMEM_SPEC] * len(shapes) if several else VMEM_SPEC,
        scratch_shapes=list(scratch),
        compiler_params=pltpu.CompilerParams(vmem_limit_bytes=limit * 1024 * 1024),
        name=name,
    )(*operands)


def held(blocks):
    return [
        pltpu.VMEM(blocks.shape, blocks.dtype),
        pltpu.SemaphoreType.DMA((blocks.shape[0] // CHUNK,)),
    ]


def as_block(values, shape):
    padding = [(0, n - m) for n, m in zip(shape, values.shape)]
    return jnp.pad(values, padding).astype(BF16)


def from_block(block, columns):
    return block[:, :columns].astype(F32).astype(jnp.int32)


def on_device(couplings, diag_blocks, coupling_cols, aggregate, pattern, tests):
    rows, vectors, width = tests.shape
    stored = couplings.shape[1]
    half = rows // 2
    slab = lax.axis_index("rows")
    slot = lax.axis_index("aggs")
    core = lax.axis_index("vecs")
    whole_shape = jax.ShapeDtypeStruct((rows, vectors, width), F32)
    extra_shape = (vectors, 2 * width)

    def folded(blocks):
        return jax.ShapeDtypeStruct((blocks, vectors, 2 * width), BF16)

    cols = coupling_cols - slab * rows + rows
    local_aggs = aggregate - slab * SLAB_AGGS
    slot_aggs = jnp.concatenate([aggregate[:, None], pattern], axis=1) - slab * SLAB_AGGS
    inside = cols[:, :, None] == jnp.arange(rows, 2 * rows, dtype=jnp.int32)
    column_aggs = jnp.sum(jnp.where(inside, local_aggs + 1, 0), axis=2) - 1
    hits = column_aggs[:, :, None] == slot_aggs[:, None, :]
    near_slot = jnp.sum(jnp.where(hits, jnp.arange(1, SLOTS + 1, dtype=jnp.int32), 0), axis=2) - 1
    ids_block = as_block(slot_aggs, extra_shape)
    slot_block = as_block(near_slot, extra_shape)
    first = jnp.where(core == 0, slot ^ 1, 3 - slot)
    second = jnp.where(core == 0, 3 - slot, slot ^ 1)
    where = jnp.stack([core, slot, slot, second, first, slot ^ 2]).astype(jnp.int32)

    folded_whole = jax.ShapeDtypeStruct((half, vectors, 2 * width), F32)
    couplings = pl.pallas_call(
        stage_kernel,
        out_shape=pltpu.VMEM((rows, width, stored * width), BF16),
        in_specs=[HBM_SPEC],
        out_specs=VMEM_SPEC,
        scratch_shapes=held(couplings),
        compiler_params=pltpu.CompilerParams(vmem_limit_bytes=12 * 1024 * 1024),
        cost_estimate=pl.CostEstimate(flops=0, bytes_accessed=8000000, transcendentals=0),
        name="stage",
    )(pltpu.with_memory_space_constraint(couplings, pltpu.HBM))
    rounded = kernel_call(fold_kernel, "fold", folded(half), [tests])
    current, scale, folded_scale, places, far_slot = tests, None, None, None, None
    for sweep in range(SWEEPS):
        last = sweep == SWEEPS - 1
        before = shift(rounded, 1)
        after = shift(rounded, -1)
        if sweep == 0:
            rest, scale, folded_scale = kernel_call(
                first_center_kernel,
                "first_center",
                [
                    folded_whole,
                    jax.ShapeDtypeStruct((rows, width), F32),
                    jax.ShapeDtypeStruct((half, 2 * width), F32),
                ],
                [diag_blocks, current],
                held(diag_blocks),
            )
        else:
            rest = kernel_call(
                folded_center_kernel,
                "center",
                folded_whole,
                [diag_blocks, current, scale],
                held(diag_blocks) + [pltpu.VMEM((rows, vectors, width), F32)],
            )
        if sweep == 1:
            places = jnp.concatenate(
                [
                    from_block(before[half], SLOTS),
                    slot_aggs + SLAB_AGGS,
                    from_block(after[half], SLOTS) + 2 * SLAB_AGGS,
                ],
                axis=0,
            )
        part = kernel_call(
            couple_kernel,
            "couple",
            folded(half + last),
            [cols, couplings, before, rounded, after] + [slot_block] * last,
            [pltpu.VMEM((3 * rows, vectors, 2 * LANES), BF16)] * 2,
        )
        far = exchange(part, 0)
        if last:
            far_slot = from_block(far[half], stored)
        pair = kernel_call(pair_kernel, "pair", folded(half), [part, far])
        operands = [rest, pair, exchange(pair, 1), folded_scale]
        if last:
            current = kernel_call(last_update_kernel, "last_update", whole_shape, operands)
        else:
            current, rounded = kernel_call(
                update_kernel,
                "update",
                [folded_whole, folded(half + (sweep == 0))],
                operands + [ids_block] * (sweep == 0),
            )

    every = lax.all_gather(current, "vecs", axis=1, tiled=True)
    grams = jnp.einsum("ivb,iwb->ivw", every, every, precision=HIGHEST_PRECISION)
    members = (local_aggs[:, None] == jnp.arange(SLAB_AGGS, dtype=jnp.int32)[None, :]).astype(F32)
    totals = jnp.einsum("ig,ivw->vwg", members, grams, precision=HIGHEST_PRECISION) / width
    inverse = kernel_call(
        inverse_factor_kernel,
        "inverse_factor",
        jax.ShapeDtypeStruct((VECTORS, VECTORS, SLAB_AGGS), F32),
        [totals],
    )
    own_inverse = lax.dynamic_slice_in_dim(inverse, core * vectors, vectors, 0)
    row_inverse = jnp.einsum("ig,cvg->icv", members, own_inverse, precision=HIGHEST_PRECISION)
    tentative = jnp.einsum("icv,ivb->icb", row_inverse, every, precision=HIGHEST_PRECISION)

    moved = kernel_call(
        fit_kernel,
        "fit",
        jax.ShapeDtypeStruct((half, stored, vectors, 2 * width), BF16),
        [cols, couplings, tentative.astype(BF16)],
        [pltpu.VMEM((rows, vectors, 2 * LANES), BF16)] * 2,
    )
    rest = kernel_call(
        center_kernel,
        "center",
        folded_whole,
        [diag_blocks, tentative, scale],
        held(diag_blocks),
    )
    slots_shape = jax.ShapeDtypeStruct((half, SLOTS, vectors, 2 * width), BF16)
    pair = kernel_call(
        slot_kernel, "slots", slots_shape, [near_slot, far_slot, moved, exchange(moved, 0)]
    )
    prolong, prolong_here = kernel_call(
        finish_kernel,
        "finish",
        [slots_shape, jax.ShapeDtypeStruct((rows, 1, vectors, width), BF16)],
        [where, rest, pair, exchange(pair, 1), folded_scale],
    )

    other = lax.ppermute(prolong, "vecs", [(0, 1), (1, 0)])
    before = shift(prolong, 1)
    after = shift(prolong, -1)
    span = 3 * SLAB_AGGS
    quarter = span * vectors // 4
    wide = SLAB_AGGS * 2 * vectors
    keep, send = kernel_call(
        coarse_kernel,
        "coarse",
        [
            jax.ShapeDtypeStruct((2, quarter, wide), F32),
            jax.ShapeDtypeStruct((2, quarter, wide), BF16),
        ],
        [where, cols, places, couplings, diag_blocks, before, prolong, after, other],
        [
            pltpu.VMEM((3 * rows, SLOTS, vectors, 2 * LANES), BF16),
            pltpu.VMEM((3 * rows, SLOTS, vectors, 2 * LANES), BF16),
            pltpu.VMEM((rows, span, vectors, width), F32),
            pltpu.VMEM((rows, 2, SLAB_AGGS, vectors, width), BF16),
            pltpu.VMEM((span * vectors, wide), F32),
        ]
        + [
            pltpu.VMEM((rows // 4, width, width), BF16),
            pltpu.SemaphoreType.DMA((1,)),
        ],
        limit=28,
    )
    merged = keep + exchange(send, 0).astype(F32)
    owned = merged[0] + exchange(merged[1].astype(BF16), 1).astype(F32)
    mine, theirs = owned[:, : wide // 2], owned[:, wide // 2 :]
    theirs = lax.ppermute(theirs, "vecs", [(0, 1), (1, 0)])
    low = jnp.where(core == 0, mine, theirs).reshape(span // 4, vectors, -1)
    high = jnp.where(core == 0, theirs, mine).reshape(span // 4, vectors, -1)
    coarse = jnp.concatenate([low, high], axis=1).reshape(span // 4, VECTORS, SLAB_AGGS, vectors)
    return (prolong_here, coarse.transpose(2, 0, 3, 1))


def solution(mesh):
    return jax.shard_map(
        on_device,
        mesh=mesh,
        in_specs=(
            P("rows", "aggs", None, None),
            P("rows", None, None),
            P("rows", "aggs"),
            P("rows"),
            P("rows", None),
            P("rows", "vecs", None),
        ),
        out_specs=(P("rows", "aggs", "vecs", None), P("rows", "aggs", "vecs", None)),
        check_vma=False,
    )
```

```python
import jax
import jax.numpy as jnp
from jax import lax
from jax.experimental import pallas as pl
from jax.experimental.pallas import tpu as pltpu
from jax.sharding import PartitionSpec as P

VECTORS = 32
SWEEPS = 3
SLAB_AGGS = 8
SLOTS = 4
DAMPING = 2.0 / 3.0
HIGHEST_PRECISION = lax.Precision.HIGHEST
BF16 = jnp.bfloat16
F32 = jnp.float32

SMEM_SPEC = pl.BlockSpec(memory_space=pltpu.SMEM)
VMEM_SPEC = pl.BlockSpec(memory_space=pltpu.VMEM)
HBM_SPEC = pl.BlockSpec(memory_space=pltpu.HBM)


def dot_nt(left, right):
    return lax.dot_general(left, right, (((1,), (1,)), ((), ())), preferred_element_type=F32)


LANES = 128


def put(ref, low, high):
    width = low.shape[-1]
    ref[:, :width] = low.astype(ref.dtype)
    ref[:, width : 2 * width - LANES] = high[:, LANES:].astype(ref.dtype)
    ref[:, 2 * width - LANES :] = high[:, :LANES].astype(ref.dtype)


def take_into(low_ref, high_ref, block):
    width = block.shape[-1] // 2
    low_ref[...] = block[:, :width]
    high_ref[:, :LANES] = block[:, 2 * width - LANES :]
    high_ref[:, LANES:] = block[:, width : 2 * width - LANES]


CHUNK = 2


def fetches(source_ref, held_ref, sems):
    half = source_ref.shape[0] // 2
    copies = []
    for c in range(half // CHUNK):
        for start in (c * CHUNK, half + c * CHUNK):
            rows = pl.ds(start, CHUNK)
            copies.append(
                pltpu.make_async_copy(
                    source_ref.at[rows], held_ref.at[rows], sems.at[len(copies)]
                )
            )
    for copy in copies:
        copy.start()

    def ready(m):
        if m % CHUNK == 0:
            for copy in copies[2 * (m // CHUNK) : 2 * (m // CHUNK) + 2]:
                copy.wait()

    return ready


def center_kernel(source_ref, x_ref, scale_ref, y_ref, diag_ref, sems, ready=None):
    half = x_ref.shape[0] // 2
    if ready is None:
        ready = fetches(source_ref, diag_ref, sems)

    def rest(i):
        x = x_ref[i]
        return x - scale_ref[i : i + 1, :] * dot_nt(x.astype(BF16), diag_ref[i])

    for m in range(half):
        ready(m)
        put(y_ref.at[m], rest(m), rest(half + m))


def folded_center_kernel(source_ref, x_ref, scale_ref, y_ref, diag_ref, sems, rows):
    half = x_ref.shape[0]
    ready = fetches(source_ref, diag_ref, sems)
    for m in range(half):
        take_into(rows.at[m], rows.at[half + m], x_ref[m])
    center_kernel(source_ref, rows, scale_ref, y_ref, diag_ref, sems, ready)


def first_center_kernel(source_ref, x_ref, y_ref, scale_ref, folded_scale_ref, diag_ref, sems):
    rows, _, width = x_ref.shape
    copy = pltpu.make_async_copy(source_ref, diag_ref, sems.at[0])
    copy.start()
    copy.wait()
    on_diagonal = lax.broadcasted_iota(jnp.int32, (width, width), 0) == lax.broadcasted_iota(
        jnp.int32, (width, width), 1
    )
    for i in range(rows):
        block = diag_ref[i].astype(F32)
        pivot = jnp.sum(jnp.where(on_diagonal, block, 0.0), axis=0, keepdims=True)
        scale_ref[i : i + 1, :] = DAMPING / pivot
    for m in range(rows // 2):
        put(
            folded_scale_ref.at[m : m + 1],
            scale_ref[m : m + 1, :],
            scale_ref[rows // 2 + m : rows // 2 + m + 1, :],
        )
    center_kernel(source_ref, x_ref, scale_ref, y_ref, diag_ref, sems, lambda m: None)


def fold_kernel(x_ref, out_ref):
    half = out_ref.shape[0]
    for m in range(half):
        put(out_ref.at[m], x_ref[m], x_ref[half + m])


def stage_kernel(source_ref, out_ref, a_ref, sems):
    half = source_ref.shape[0] // 2
    ready = fetches(source_ref, a_ref, sems)
    for m in range(half):
        ready(m)
        for i in (m, half + m):
            put(out_ref.at[i], a_ref[i, 0], a_ref[i, 1])


def spread(low_ref, high_ref, main, rest):
    zero = jnp.zeros_like(rest)
    low_ref[:, :LANES] = main
    low_ref[:, LANES:] = jnp.concatenate([rest, zero], axis=1)
    high_ref[:, LANES:] = main
    high_ref[:, :LANES] = jnp.concatenate([zero, rest], axis=1)


def spread_folded(low_ref, high_ref, first, second, block):
    wide = block.shape[-1]
    width = wide // 2
    spread(low_ref.at[first], high_ref.at[first], block[:, :LANES], block[:, LANES:width])
    spread(
        low_ref.at[second],
        high_ref.at[second],
        block[:, wide - LANES :],
        block[:, width : wide - LANES],
    )


def joined(low, high):
    return jnp.concatenate(
        [low[:, :LANES], low[:, LANES:] + high[:, :LANES], high[:, LANES:]], axis=1
    )


def stacked(low, high):
    zero = jnp.zeros((low.shape[0], LANES), low.dtype)
    return jnp.concatenate(
        [jnp.concatenate([low, zero], axis=1), jnp.concatenate([zero, high], axis=1)], axis=0
    )


def pair_kernel(near_ref, far_ref, out_ref):
    for m in range(out_ref.shape[0]):
        out_ref[m] = (near_ref[m].astype(F32) + far_ref[m].astype(F32)).astype(BF16)


def updated(m, rest_ref, near_ref, far_ref, scale_ref):
    total = near_ref[m].astype(F32) + far_ref[m].astype(F32)
    return rest_ref[m] - scale_ref[m : m + 1, :] * total


def update_kernel(rest_ref, near_ref, far_ref, scale_ref, *refs):
    half = rest_ref.shape[0]
    extra_ref = refs[0] if len(refs) == 3 else None
    x_ref, rounded_ref = refs[-2:]
    for m in range(half):
        x = updated(m, rest_ref, near_ref, far_ref, scale_ref)
        x_ref[m] = x
        rounded_ref[m] = x.astype(BF16)
    if extra_ref is not None:
        rounded_ref[half] = extra_ref[...]


def last_update_kernel(rest_ref, near_ref, far_ref, scale_ref, x_ref):
    half = rest_ref.shape[0]
    for m in range(half):
        x = updated(m, rest_ref, near_ref, far_ref, scale_ref)
        take_into(x_ref.at[m], x_ref.at[half + m], x)


def couple_kernel(col_ref, a_ref, before_ref, own_ref, after_ref, *refs):
    rows = a_ref.shape[0]
    half = rows // 2
    extra_ref = refs[0] if len(refs) == 4 else None
    out_ref, low, high = refs[-3:]
    for s, ref in enumerate((before_ref, own_ref, after_ref)):
        for m in range(half):
            spread_folded(low, high, s * rows + m, s * rows + half + m, ref[m])

    def product(i):
        return dot_nt(joined(low[col_ref[i, 0]], high[col_ref[i, 1]]), a_ref[i])

    for m in range(half):
        put(out_ref.at[m], product(m), product(half + m))
    if extra_ref is not None:
        out_ref[half] = extra_ref[...]


def fit_kernel(col_ref, a_ref, own_ref, out_ref, low, high):
    rows, vectors, width = own_ref.shape
    half = rows // 2
    for i in range(rows):
        own = own_ref[i]
        spread(low.at[i], high.at[i], own[:, :LANES], own[:, LANES:])

    def products(i):
        first, second = (jnp.clip(col_ref[i, k] - rows, 0, rows - 1) for k in range(2))
        return dot_nt(stacked(low[first], high[second]), a_ref[i])

    for m in range(half):
        near, far = products(m), products(half + m)
        for k in range(2):
            part = slice(k * vectors, (k + 1) * vectors)
            put(out_ref.at[m, k], near[part], far[part])


def slot_kernel(slot_ref, far_slot_ref, near_ref, far_ref, out_ref):
    half, stored, vectors, wide = near_ref.shape
    is_low = lax.broadcasted_iota(jnp.int32, (vectors, wide), 1) < wide // 2
    for m in range(half):
        terms = []
        for ids_ref, ref in ((slot_ref, near_ref), (far_slot_ref, far_ref)):
            for k in range(stored):
                ids = jnp.where(is_low, ids_ref[m, k], ids_ref[half + m, k])
                terms.append((ids, ref[m, k].astype(F32)))
        for p in range(SLOTS):
            total = jnp.zeros((vectors, wide), F32)
            for ids, value in terms:
                total = total + jnp.where(ids == p, value, 0.0)
            out_ref[m, p] = total.astype(BF16)


def finish_kernel(rest_ref, near_ref, far_ref, scale_ref, out_ref):
    for m in range(rest_ref.shape[0]):
        scale = scale_ref[m : m + 1, :]
        for p in range(SLOTS):
            total = near_ref[m, p].astype(F32) + far_ref[m, p].astype(F32)
            value = -scale * total
            if p == 0:
                value = rest_ref[m] + value
            out_ref[m, p] = value.astype(BF16)


def here_kernel(where_ref, prolong_ref, here_ref):
    half = prolong_ref.shape[0]
    for m in range(half):
        take_into(here_ref.at[m, 0], here_ref.at[half + m, 0], prolong_ref[m, where_ref[1]])


def inverse_factor_kernel(m_ref, out_ref):
    size = m_ref.shape[0]
    rows = [m_ref[v] for v in range(size)]
    place = lax.broadcasted_iota(jnp.int32, rows[0].shape, 0)
    for k in range(size):
        root = lax.rsqrt(rows[k][k : k + 1, :])
        here = place == k
        pivot_row = jnp.where(here, root, rows[k] * root)
        rows[k] = jnp.where(place <= k, pivot_row, 0.0)
        out_ref[k] = rows[k]
        for v in range(k + 1, size):
            rows[v] = jnp.where(here, 0.0, rows[v]) - pivot_row[v : v + 1, :] * pivot_row


def coarse_kernel(
    where_ref, col_ref, place_ref, a_ref, diag_source_ref, before_ref, own_ref, after_ref, other_ref,
    keep_ref, send_ref, low, high, reach, left, total, diag_ref, diag_sem,
):
    rows, width = a_ref.shape[:2]
    vectors = own_ref.shape[2]
    share = rows // 4
    slot = where_ref[1]
    span = reach.shape[0]
    diag_copy = pltpu.make_async_copy(
        diag_source_ref.at[pl.ds(slot * share, share)], diag_ref, diag_sem.at[0]
    )
    diag_copy.start()
    reach[...] = jnp.zeros_like(reach)
    left[...] = jnp.zeros_like(left)

    half = rows // 2
    for s, ref in enumerate((before_ref, own_ref, after_ref)):
        for m in range(half):
            for p in range(SLOTS):
                spread_folded(
                    low.at[:, p], high.at[:, p], s * rows + m, s * rows + half + m, ref[m, p]
                )

    span_rows = SLOTS * vectors

    def add(lanes, row, image, fresh):
        places = [place_ref[row, q] for q in range(SLOTS)]
        zero = jnp.zeros((span_rows, 2 * LANES - width), F32)
        image = jnp.concatenate([image, zero], axis=1)
        blocks = [image[q * vectors : (q + 1) * vectors] for q in range(SLOTS)]
        if not fresh:
            held_now = [reach[at, :, lanes] for at in places]
            blocks = [block + now for block, now in zip(blocks, held_now)]
        for at, block in zip(places, blocks):
            reach[at, :, lanes] = block

    def lanes_of(i):
        if isinstance(i, int):
            return slice(i * 2 * LANES, (i + 1) * 2 * LANES)
        return pl.ds(pl.multiple_of(i * 2 * LANES, LANES), 2 * LANES)

    for m in range(half):
        low_lanes, high_lanes = lanes_of(m), lanes_of(half + m)
        for p in range(SLOTS):
            first = place_ref[rows + m, p] - SLAB_AGGS
            second = place_ref[rows + half + m, p] - SLAB_AGGS
            left[0, first, :, low_lanes] = low[rows + m, p]
            left[0, second, :, high_lanes] = low[rows + half + m, p]
            block = other_ref[m, p]
            zero = jnp.zeros((vectors, 2 * LANES - width), BF16)
            left[1, first, :, low_lanes] = jnp.concatenate([block[:, :width], zero], axis=1)
            left[1, second, :, high_lanes] = jnp.concatenate(
                [block[:, 2 * width - LANES :], block[:, width : 2 * width - LANES], zero], axis=1
            )
    for i in range(rows):
        first, second = col_ref[i, 0], col_ref[i, 1]
        images = dot_nt(
            stacked(
                low[first].reshape(span_rows, 2 * LANES),
                high[second].reshape(span_rows, 2 * LANES),
            ),
            a_ref[i],
        )
        add(lanes_of(i), first, images[:span_rows], True)
        add(lanes_of(i), second, images[span_rows:], False)

    diag_copy.wait()
    for r in range(share):
        i = slot * share + r
        own = low[rows + i].reshape(span_rows, 2 * LANES)[:, :width]
        add(lanes_of(i), rows + i, dot_nt(own, diag_ref[r]), False)

    depth = 4 * 2 * LANES
    for c in range(rows // 4):
        lanes = slice(c * depth, (c + 1) * depth)
        product = dot_nt(
            reach[:, :, lanes].astype(BF16).reshape(span * vectors, depth),
            left[:, :, :, lanes].reshape(2 * SLAB_AGGS * vectors, depth),
        )
        if c == 0:
            total[...] = product
        else:
            total[...] = total[...] + product
    quarter = span * vectors // 4
    for n in range(2):
        start = pl.multiple_of(where_ref[2 + n] * quarter, 32)
        keep_ref[n] = total[pl.ds(start, quarter), :] * (1.0 / width)
        start = pl.multiple_of(where_ref[4 + n] * quarter, 32)
        send_ref[n] = (total[pl.ds(start, quarter), :] * (1.0 / width)).astype(BF16)


def shift(x, by):
    size = lax.axis_size("rows")
    return lax.ppermute(x, "rows", [(i, i + by) for i in range(size) if 0 <= i + by < size])


def partner(slot, core, phase):
    return slot ^ 1 if (core + phase) % 2 == 0 else 3 - slot


def exchange(x, phase):
    pairs = [(2 * s + c, 2 * partner(s, c, phase) + c) for s in range(4) for c in range(2)]
    return lax.ppermute(x, ("aggs", "vecs"), pairs)


def kernel_call(body, name, shapes, operands, scratch=(), limit=12):
    several = isinstance(shapes, list)
    is_block = [x.ndim == 3 and x.shape[-1] == x.shape[-2] and x.dtype == BF16 for x in operands]
    specs = [
        SMEM_SPEC if x.dtype == jnp.int32 else HBM_SPEC if block else VMEM_SPEC
        for x, block in zip(operands, is_block)
    ]
    operands = [
        pltpu.with_memory_space_constraint(x, pltpu.HBM) if block else x
        for x, block in zip(operands, is_block)
    ]
    return pl.pallas_call(
        body,
        out_shape=shapes,
        in_specs=specs,
        out_specs=[VMEM_SPEC] * len(shapes) if several else VMEM_SPEC,
        scratch_shapes=list(scratch),
        compiler_params=pltpu.CompilerParams(vmem_limit_bytes=limit * 1024 * 1024),
        name=name,
    )(*operands)


def held(blocks):
    return [
        pltpu.VMEM(blocks.shape, blocks.dtype),
        pltpu.SemaphoreType.DMA((blocks.shape[0] // CHUNK,)),
    ]


def as_block(values, shape):
    padding = [(0, n - m) for n, m in zip(shape, values.shape)]
    return jnp.pad(values, padding).astype(BF16)


def from_block(block, columns):
    return block[:, :columns].astype(F32).astype(jnp.int32)


def on_device(couplings, diag_blocks, coupling_cols, aggregate, pattern, tests):
    rows, vectors, width = tests.shape
    stored = couplings.shape[1]
    half = rows // 2
    slab = lax.axis_index("rows")
    slot = lax.axis_index("aggs")
    core = lax.axis_index("vecs")
    whole_shape = jax.ShapeDtypeStruct((rows, vectors, width), F32)
    extra_shape = (vectors, 2 * width)

    def folded(blocks):
        return jax.ShapeDtypeStruct((blocks, vectors, 2 * width), BF16)

    cols = coupling_cols - slab * rows + rows
    local_aggs = aggregate - slab * SLAB_AGGS
    slot_aggs = jnp.concatenate([aggregate[:, None], pattern], axis=1) - slab * SLAB_AGGS
    inside = cols[:, :, None] == jnp.arange(rows, 2 * rows, dtype=jnp.int32)
    column_aggs = jnp.sum(jnp.where(inside, local_aggs + 1, 0), axis=2) - 1
    hits = column_aggs[:, :, None] == slot_aggs[:, None, :]
    near_slot = jnp.sum(jnp.where(hits, jnp.arange(1, SLOTS + 1, dtype=jnp.int32), 0), axis=2) - 1
    ids_block = as_block(slot_aggs, extra_shape)
    slot_block = as_block(near_slot, extra_shape)
    first = jnp.where(core == 0, slot ^ 1, 3 - slot)
    second = jnp.where(core == 0, 3 - slot, slot ^ 1)
    where = jnp.stack([core, slot, slot, second, first, slot ^ 2]).astype(jnp.int32)

    folded_whole = jax.ShapeDtypeStruct((half, vectors, 2 * width), F32)
    couplings = pl.pallas_call(
        stage_kernel,
        out_shape=pltpu.VMEM((rows, width, stored * width), BF16),
        in_specs=[HBM_SPEC],
        out_specs=VMEM_SPEC,
        scratch_shapes=held(couplings),
        compiler_params=pltpu.CompilerParams(vmem_limit_bytes=12 * 1024 * 1024),
        cost_estimate=pl.CostEstimate(flops=0, bytes_accessed=8000000, transcendentals=0),
        name="stage",
    )(pltpu.with_memory_space_constraint(couplings, pltpu.HBM))
    rounded = kernel_call(fold_kernel, "fold", folded(half), [tests])
    current, scale, folded_scale, places, far_slot = tests, None, None, None, None
    for sweep in range(SWEEPS):
        last = sweep == SWEEPS - 1
        before = shift(rounded, 1)
        after = shift(rounded, -1)
        if sweep == 0:
            rest, scale, folded_scale = kernel_call(
                first_center_kernel,
                "first_center",
                [
                    folded_whole,
                    jax.ShapeDtypeStruct((rows, width), F32),
                    jax.ShapeDtypeStruct((half, 2 * width), F32),
                ],
                [diag_blocks, current],
                held(diag_blocks),
            )
        else:
            rest = kernel_call(
                folded_center_kernel,
                "center",
                folded_whole,
                [diag_blocks, current, scale],
                held(diag_blocks) + [pltpu.VMEM((rows, vectors, width), F32)],
            )
        if sweep == 1:
            places = jnp.concatenate(
                [
                    from_block(before[half], SLOTS),
                    slot_aggs + SLAB_AGGS,
                    from_block(after[half], SLOTS) + 2 * SLAB_AGGS,
                ],
                axis=0,
            )
        part = kernel_call(
            couple_kernel,
            "couple",
            folded(half + last),
            [cols, couplings, before, rounded, after] + [slot_block] * last,
            [pltpu.VMEM((3 * rows, vectors, 2 * LANES), BF16)] * 2,
        )
        far = exchange(part, 0)
        if last:
            far_slot = from_block(far[half], stored)
        pair = kernel_call(pair_kernel, "pair", folded(half), [part, far])
        operands = [rest, pair, exchange(pair, 1), folded_scale]
        if last:
            current = kernel_call(last_update_kernel, "last_update", whole_shape, operands)
        else:
            current, rounded = kernel_call(
                update_kernel,
                "update",
                [folded_whole, folded(half + (sweep == 0))],
                operands + [ids_block] * (sweep == 0),
            )

    every = lax.all_gather(current, "vecs", axis=1, tiled=True)
    grams = jnp.einsum("ivb,iwb->ivw", every, every, precision=HIGHEST_PRECISION)
    members = (local_aggs[:, None] == jnp.arange(SLAB_AGGS, dtype=jnp.int32)[None, :]).astype(F32)
    totals = jnp.einsum("ig,ivw->vwg", members, grams, precision=HIGHEST_PRECISION) / width
    inverse = kernel_call(
        inverse_factor_kernel,
        "inverse_factor",
        jax.ShapeDtypeStruct((VECTORS, VECTORS, SLAB_AGGS), F32),
        [totals],
    )
    own_inverse = lax.dynamic_slice_in_dim(inverse, core * vectors, vectors, 0)
    row_inverse = jnp.einsum("ig,cvg->icv", members, own_inverse, precision=HIGHEST_PRECISION)
    tentative = jnp.einsum("icv,ivb->icb", row_inverse, every, precision=HIGHEST_PRECISION)

    moved = kernel_call(
        fit_kernel,
        "fit",
        jax.ShapeDtypeStruct((half, stored, vectors, 2 * width), BF16),
        [cols, couplings, tentative.astype(BF16)],
        [pltpu.VMEM((rows, vectors, 2 * LANES), BF16)] * 2,
    )
    rest = kernel_call(
        center_kernel,
        "center",
        folded_whole,
        [diag_blocks, tentative, scale],
        held(diag_blocks),
    )
    slots_shape = jax.ShapeDtypeStruct((half, SLOTS, vectors, 2 * width), BF16)
    pair = kernel_call(
        slot_kernel, "slots", slots_shape, [near_slot, far_slot, moved, exchange(moved, 0)]
    )
    prolong = kernel_call(
        finish_kernel, "finish", slots_shape, [rest, pair, exchange(pair, 1), folded_scale]
    )
    prolong_here = kernel_call(
        here_kernel,
        "here",
        jax.ShapeDtypeStruct((rows, 1, vectors, width), BF16),
        [where, prolong],
    )

    other = lax.ppermute(prolong, "vecs", [(0, 1), (1, 0)])
    before = shift(prolong, 1)
    after = shift(prolong, -1)
    span = 3 * SLAB_AGGS
    quarter = span * vectors // 4
    wide = SLAB_AGGS * 2 * vectors
    keep, send = kernel_call(
        coarse_kernel,
        "coarse",
        [
            jax.ShapeDtypeStruct((2, quarter, wide), F32),
            jax.ShapeDtypeStruct((2, quarter, wide), BF16),
        ],
        [where, cols, places, couplings, diag_blocks, before, prolong, after, other],
        [
            pltpu.VMEM((3 * rows, SLOTS, vectors, 2 * LANES), BF16),
            pltpu.VMEM((3 * rows, SLOTS, vectors, 2 * LANES), BF16),
            pltpu.VMEM((span, vectors, rows * 2 * LANES), F32),
            pltpu.VMEM((2, SLAB_AGGS, vectors, rows * 2 * LANES), BF16),
            pltpu.VMEM((span * vectors, wide), F32),
        ]
        + [
            pltpu.VMEM((rows // 4, width, width), BF16),
            pltpu.SemaphoreType.DMA((1,)),
        ],
        limit=28,
    )
    merged = keep + exchange(send, 0).astype(F32)
    owned = merged[0] + exchange(merged[1].astype(BF16), 1).astype(F32)
    mine, theirs = owned[:, : wide // 2], owned[:, wide // 2 :]
    theirs = lax.ppermute(theirs, "vecs", [(0, 1), (1, 0)])
    low = jnp.where(core == 0, mine, theirs).reshape(span // 4, vectors, -1)
    high = jnp.where(core == 0, theirs, mine).reshape(span // 4, vectors, -1)
    coarse = jnp.concatenate([low, high], axis=1).reshape(span // 4, VECTORS, SLAB_AGGS, vectors)
    return (prolong_here, coarse.transpose(2, 0, 3, 1))


def solution(mesh):
    return jax.shard_map(
        on_device,
        mesh=mesh,
        in_specs=(
            P("rows", "aggs", None, None),
            P("rows", None, None),
            P("rows", "aggs"),
            P("rows"),
            P("rows", None),
            P("rows", "vecs", None),
        ),
        out_specs=(P("rows", "aggs", "vecs", None), P("rows", "aggs", "vecs", None)),
        check_vma=False,
    )
```

```python
import jax
import jax.numpy as jnp
from jax import lax
from jax.experimental import pallas as pl
from jax.experimental.pallas import tpu as pltpu
from jax.sharding import PartitionSpec as P

VECTORS = 32
SWEEPS = 3
SLAB_AGGS = 8
SLOTS = 4
DAMPING = 2.0 / 3.0
HIGHEST_PRECISION = lax.Precision.HIGHEST
BF16 = jnp.bfloat16
F32 = jnp.float32

SMEM_SPEC = pl.BlockSpec(memory_space=pltpu.SMEM)
VMEM_SPEC = pl.BlockSpec(memory_space=pltpu.VMEM)
HBM_SPEC = pl.BlockSpec(memory_space=pltpu.HBM)


def dot_nt(left, right):
    return lax.dot_general(left, right, (((1,), (1,)), ((), ())), preferred_element_type=F32)


LANES = 128


def put(ref, low, high):
    width = low.shape[-1]
    ref[:, :width] = low.astype(ref.dtype)
    ref[:, width : 2 * width - LANES] = high[:, LANES:].astype(ref.dtype)
    ref[:, 2 * width - LANES :] = high[:, :LANES].astype(ref.dtype)


def take_into(low_ref, high_ref, block):
    width = block.shape[-1] // 2
    low_ref[...] = block[:, :width]
    high_ref[:, :LANES] = block[:, 2 * width - LANES :]
    high_ref[:, LANES:] = block[:, width : 2 * width - LANES]


CHUNK = 2


def fetches(source_ref, held_ref, sems):
    half = source_ref.shape[0] // 2
    copies = []
    for c in range(half // CHUNK):
        for start in (c * CHUNK, half + c * CHUNK):
            rows = pl.ds(start, CHUNK)
            copies.append(
                pltpu.make_async_copy(
                    source_ref.at[rows], held_ref.at[rows], sems.at[len(copies)]
                )
            )
    for copy in copies:
        copy.start()

    def ready(m):
        if m % CHUNK == 0:
            for copy in copies[2 * (m // CHUNK) : 2 * (m // CHUNK) + 2]:
                copy.wait()

    return ready


def center_kernel(source_ref, x_ref, scale_ref, y_ref, diag_ref, sems, ready=None):
    half = x_ref.shape[0] // 2
    if ready is None:
        ready = fetches(source_ref, diag_ref, sems)

    def rest(i):
        x = x_ref[i]
        return x - scale_ref[i : i + 1, :] * dot_nt(x.astype(BF16), diag_ref[i])

    for m in range(half):
        ready(m)
        put(y_ref.at[m], rest(m), rest(half + m))


def folded_center_kernel(source_ref, x_ref, scale_ref, y_ref, diag_ref, sems, rows):
    half = x_ref.shape[0]
    ready = fetches(source_ref, diag_ref, sems)
    for m in range(half):
        take_into(rows.at[m], rows.at[half + m], x_ref[m])
    center_kernel(source_ref, rows, scale_ref, y_ref, diag_ref, sems, ready)


def first_center_kernel(source_ref, x_ref, y_ref, scale_ref, folded_scale_ref, diag_ref, sems):
    rows, _, width = x_ref.shape
    copy = pltpu.make_async_copy(source_ref, diag_ref, sems.at[0])
    copy.start()
    copy.wait()
    on_diagonal = lax.broadcasted_iota(jnp.int32, (width, width), 0) == lax.broadcasted_iota(
        jnp.int32, (width, width), 1
    )
    for i in range(rows):
        block = diag_ref[i].astype(F32)
        pivot = jnp.sum(jnp.where(on_diagonal, block, 0.0), axis=0, keepdims=True)
        scale_ref[i : i + 1, :] = DAMPING / pivot
    for m in range(rows // 2):
        put(
            folded_scale_ref.at[m : m + 1],
            scale_ref[m : m + 1, :],
            scale_ref[rows // 2 + m : rows // 2 + m + 1, :],
        )
    center_kernel(source_ref, x_ref, scale_ref, y_ref, diag_ref, sems, lambda m: None)


def fold_kernel(x_ref, out_ref):
    half = out_ref.shape[0]
    for m in range(half):
        put(out_ref.at[m], x_ref[m], x_ref[half + m])


def stage_kernel(source_ref, out_ref, a_ref, sems):
    half = source_ref.shape[0] // 2
    ready = fetches(source_ref, a_ref, sems)
    for m in range(half):
        ready(m)
        for i in (m, half + m):
            put(out_ref.at[i], a_ref[i, 0], a_ref[i, 1])


def spread(low_ref, high_ref, main, rest):
    zero = jnp.zeros_like(rest)
    low_ref[:, :LANES] = main
    low_ref[:, LANES:] = jnp.concatenate([rest, zero], axis=1)
    high_ref[:, LANES:] = main
    high_ref[:, :LANES] = jnp.concatenate([zero, rest], axis=1)


def spread_folded(low_ref, high_ref, first, second, block):
    wide = block.shape[-1]
    width = wide // 2
    spread(low_ref.at[first], high_ref.at[first], block[:, :LANES], block[:, LANES:width])
    spread(
        low_ref.at[second],
        high_ref.at[second],
        block[:, wide - LANES :],
        block[:, width : wide - LANES],
    )


def joined(low, high):
    return jnp.concatenate(
        [low[:, :LANES], low[:, LANES:] + high[:, :LANES], high[:, LANES:]], axis=1
    )


def stacked(low, high):
    zero = jnp.zeros((low.shape[0], LANES), low.dtype)
    return jnp.concatenate(
        [jnp.concatenate([low, zero], axis=1), jnp.concatenate([zero, high], axis=1)], axis=0
    )


def pair_kernel(near_ref, far_ref, out_ref):
    for m in range(out_ref.shape[0]):
        out_ref[m] = (near_ref[m].astype(F32) + far_ref[m].astype(F32)).astype(BF16)


def updated(m, rest_ref, near_ref, far_ref, scale_ref):
    total = near_ref[m].astype(F32) + far_ref[m].astype(F32)
    return rest_ref[m] - scale_ref[m : m + 1, :] * total


def update_kernel(rest_ref, near_ref, far_ref, scale_ref, *refs):
    half = rest_ref.shape[0]
    extra_ref = refs[0] if len(refs) == 3 else None
    x_ref, rounded_ref = refs[-2:]
    for m in range(half):
        x = updated(m, rest_ref, near_ref, far_ref, scale_ref)
        x_ref[m] = x
        rounded_ref[m] = x.astype(BF16)
    if extra_ref is not None:
        rounded_ref[half] = extra_ref[...]


def last_update_kernel(rest_ref, near_ref, far_ref, scale_ref, x_ref):
    half = rest_ref.shape[0]
    for m in range(half):
        x = updated(m, rest_ref, near_ref, far_ref, scale_ref)
        take_into(x_ref.at[m], x_ref.at[half + m], x)


def couple_kernel(col_ref, a_ref, before_ref, own_ref, after_ref, *refs):
    rows = a_ref.shape[0]
    half = rows // 2
    extra_ref = refs[0] if len(refs) == 4 else None
    out_ref, low, high = refs[-3:]
    for s, ref in enumerate((before_ref, own_ref, after_ref)):
        for m in range(half):
            spread_folded(low, high, s * rows + m, s * rows + half + m, ref[m])

    def product(i):
        return dot_nt(joined(low[col_ref[i, 0]], high[col_ref[i, 1]]), a_ref[i])

    for m in range(half):
        put(out_ref.at[m], product(m), product(half + m))
    if extra_ref is not None:
        out_ref[half] = extra_ref[...]


def fit_kernel(col_ref, a_ref, own_ref, out_ref, low, high):
    rows, vectors, width = own_ref.shape
    half = rows // 2
    for i in range(rows):
        own = own_ref[i]
        spread(low.at[i], high.at[i], own[:, :LANES], own[:, LANES:])

    def products(i):
        first, second = (jnp.clip(col_ref[i, k] - rows, 0, rows - 1) for k in range(2))
        return dot_nt(stacked(low[first], high[second]), a_ref[i])

    for m in range(half):
        near, far = products(m), products(half + m)
        for k in range(2):
            part = slice(k * vectors, (k + 1) * vectors)
            put(out_ref.at[m, k], near[part], far[part])


def slot_kernel(slot_ref, far_slot_ref, near_ref, far_ref, out_ref):
    half, stored, vectors, wide = near_ref.shape
    is_low = lax.broadcasted_iota(jnp.int32, (vectors, wide), 1) < wide // 2
    for m in range(half):
        terms = []
        for ids_ref, ref in ((slot_ref, near_ref), (far_slot_ref, far_ref)):
            for k in range(stored):
                ids = jnp.where(is_low, ids_ref[m, k], ids_ref[half + m, k])
                terms.append((ids, ref[m, k].astype(F32)))
        for p in range(SLOTS):
            total = jnp.zeros((vectors, wide), F32)
            for ids, value in terms:
                total = total + jnp.where(ids == p, value, 0.0)
            out_ref[m, p] = total.astype(BF16)


def finish_kernel(rest_ref, near_ref, far_ref, scale_ref, out_ref):
    for m in range(rest_ref.shape[0]):
        scale = scale_ref[m : m + 1, :]
        for p in range(SLOTS):
            total = near_ref[m, p].astype(F32) + far_ref[m, p].astype(F32)
            value = -scale * total
            if p == 0:
                value = rest_ref[m] + value
            out_ref[m, p] = value.astype(BF16)


def here_kernel(where_ref, prolong_ref, here_ref):
    half = prolong_ref.shape[0]
    for m in range(half):
        take_into(here_ref.at[m, 0], here_ref.at[half + m, 0], prolong_ref[m, where_ref[1]])


def inverse_factor_kernel(m_ref, out_ref):
    size = m_ref.shape[0]
    rows = [m_ref[v] for v in range(size)]
    place = lax.broadcasted_iota(jnp.int32, rows[0].shape, 0)
    for k in range(size):
        root = lax.rsqrt(rows[k][k : k + 1, :])
        here = place == k
        pivot_row = jnp.where(here, root, rows[k] * root)
        rows[k] = jnp.where(place <= k, pivot_row, 0.0)
        out_ref[k] = rows[k]
        for v in range(k + 1, size):
            rows[v] = jnp.where(here, 0.0, rows[v]) - pivot_row[v : v + 1, :] * pivot_row


def coarse_kernel(
    where_ref, col_ref, place_ref, a_ref, diag_source_ref, before_ref, own_ref, after_ref, other_ref,
    keep_ref, send_ref, low, high, reach, left, total, diag_ref, diag_sem,
):
    rows, width = a_ref.shape[:2]
    vectors = own_ref.shape[2]
    share = rows // 4
    slot = where_ref[1]
    span = reach.shape[0]
    diag_copy = pltpu.make_async_copy(
        diag_source_ref.at[pl.ds(slot * share, share)], diag_ref, diag_sem.at[0]
    )
    diag_copy.start()
    reach[...] = jnp.zeros_like(reach)
    left[...] = jnp.zeros_like(left)

    half = rows // 2
    for s, ref in enumerate((before_ref, own_ref, after_ref)):
        for m in range(half):
            for p in range(SLOTS):
                spread_folded(
                    low.at[:, p], high.at[:, p], s * rows + m, s * rows + half + m, ref[m, p]
                )

    span_rows = SLOTS * vectors

    def add(lanes, row, image, fresh):
        places = [place_ref[row, q] for q in range(SLOTS)]
        zero = jnp.zeros((span_rows, 2 * LANES - width), F32)
        image = jnp.concatenate([image, zero], axis=1)
        blocks = [image[q * vectors : (q + 1) * vectors] for q in range(SLOTS)]
        if not fresh:
            held_now = [reach[at, :, lanes].astype(F32) for at in places]
            blocks = [block + now for block, now in zip(blocks, held_now)]
        for at, block in zip(places, blocks):
            reach[at, :, lanes] = block.astype(BF16)

    def lanes_of(i):
        if isinstance(i, int):
            return slice(i * 2 * LANES, (i + 1) * 2 * LANES)
        return pl.ds(pl.multiple_of(i * 2 * LANES, LANES), 2 * LANES)

    for m in range(half):
        low_lanes, high_lanes = lanes_of(m), lanes_of(half + m)
        for p in range(SLOTS):
            first = place_ref[rows + m, p] - SLAB_AGGS
            second = place_ref[rows + half + m, p] - SLAB_AGGS
            left[0, first, :, low_lanes] = low[rows + m, p]
            left[0, second, :, high_lanes] = low[rows + half + m, p]
            block = other_ref[m, p]
            zero = jnp.zeros((vectors, 2 * LANES - width), BF16)
            left[1, first, :, low_lanes] = jnp.concatenate([block[:, :width], zero], axis=1)
            left[1, second, :, high_lanes] = jnp.concatenate(
                [block[:, 2 * width - LANES :], block[:, width : 2 * width - LANES], zero], axis=1
            )
    for i in range(rows):
        first, second = col_ref[i, 0], col_ref[i, 1]
        images = dot_nt(
            stacked(
                low[first].reshape(span_rows, 2 * LANES),
                high[second].reshape(span_rows, 2 * LANES),
            ),
            a_ref[i],
        )
        add(lanes_of(i), first, images[:span_rows], True)
        add(lanes_of(i), second, images[span_rows:], False)

    diag_copy.wait()
    for r in range(share):
        i = slot * share + r
        own = low[rows + i].reshape(span_rows, 2 * LANES)[:, :width]
        add(lanes_of(i), rows + i, dot_nt(own, diag_ref[r]), False)

    depth = 4 * 2 * LANES
    for c in range(rows // 4):
        lanes = slice(c * depth, (c + 1) * depth)
        product = dot_nt(
            reach[:, :, lanes].reshape(span * vectors, depth),
            left[:, :, :, lanes].reshape(2 * SLAB_AGGS * vectors, depth),
        )
        if c == 0:
            total[...] = product
        else:
            total[...] = total[...] + product
    quarter = span * vectors // 4
    for n in range(2):
        start = pl.multiple_of(where_ref[2 + n] * quarter, 32)
        keep_ref[n] = total[pl.ds(start, quarter), :] * (1.0 / width)
        start = pl.multiple_of(where_ref[4 + n] * quarter, 32)
        send_ref[n] = (total[pl.ds(start, quarter), :] * (1.0 / width)).astype(BF16)


def shift(x, by):
    size = lax.axis_size("rows")
    return lax.ppermute(x, "rows", [(i, i + by) for i in range(size) if 0 <= i + by < size])


def partner(slot, core, phase):
    return slot ^ 1 if (core + phase) % 2 == 0 else 3 - slot


def exchange(x, phase):
    pairs = [(2 * s + c, 2 * partner(s, c, phase) + c) for s in range(4) for c in range(2)]
    return lax.ppermute(x, ("aggs", "vecs"), pairs)


def kernel_call(body, name, shapes, operands, scratch=(), limit=12):
    several = isinstance(shapes, list)
    is_block = [x.ndim == 3 and x.shape[-1] == x.shape[-2] and x.dtype == BF16 for x in operands]
    specs = [
        SMEM_SPEC if x.dtype == jnp.int32 else HBM_SPEC if block else VMEM_SPEC
        for x, block in zip(operands, is_block)
    ]
    operands = [
        pltpu.with_memory_space_constraint(x, pltpu.HBM) if block else x
        for x, block in zip(operands, is_block)
    ]
    return pl.pallas_call(
        body,
        out_shape=shapes,
        in_specs=specs,
        out_specs=[VMEM_SPEC] * len(shapes) if several else VMEM_SPEC,
        scratch_shapes=list(scratch),
        compiler_params=pltpu.CompilerParams(vmem_limit_bytes=limit * 1024 * 1024),
        name=name,
    )(*operands)


def held(blocks):
    return [
        pltpu.VMEM(blocks.shape, blocks.dtype),
        pltpu.SemaphoreType.DMA((blocks.shape[0] // CHUNK,)),
    ]


def as_block(values, shape):
    padding = [(0, n - m) for n, m in zip(shape, values.shape)]
    return jnp.pad(values, padding).astype(BF16)


def from_block(block, columns):
    return block[:, :columns].astype(F32).astype(jnp.int32)


def on_device(couplings, diag_blocks, coupling_cols, aggregate, pattern, tests):
    rows, vectors, width = tests.shape
    stored = couplings.shape[1]
    half = rows // 2
    slab = lax.axis_index("rows")
    slot = lax.axis_index("aggs")
    core = lax.axis_index("vecs")
    whole_shape = jax.ShapeDtypeStruct((rows, vectors, width), F32)
    extra_shape = (vectors, 2 * width)

    def folded(blocks):
        return jax.ShapeDtypeStruct((blocks, vectors, 2 * width), BF16)

    cols = coupling_cols - slab * rows + rows
    local_aggs = aggregate - slab * SLAB_AGGS
    slot_aggs = jnp.concatenate([aggregate[:, None], pattern], axis=1) - slab * SLAB_AGGS
    inside = cols[:, :, None] == jnp.arange(rows, 2 * rows, dtype=jnp.int32)
    column_aggs = jnp.sum(jnp.where(inside, local_aggs + 1, 0), axis=2) - 1
    hits = column_aggs[:, :, None] == slot_aggs[:, None, :]
    near_slot = jnp.sum(jnp.where(hits, jnp.arange(1, SLOTS + 1, dtype=jnp.int32), 0), axis=2) - 1
    ids_block = as_block(slot_aggs, extra_shape)
    slot_block = as_block(near_slot, extra_shape)
    first = jnp.where(core == 0, slot ^ 1, 3 - slot)
    second = jnp.where(core == 0, 3 - slot, slot ^ 1)
    where = jnp.stack([core, slot, slot, second, first, slot ^ 2]).astype(jnp.int32)

    folded_whole = jax.ShapeDtypeStruct((half, vectors, 2 * width), F32)
    couplings = pl.pallas_call(
        stage_kernel,
        out_shape=pltpu.VMEM((rows, width, stored * width), BF16),
        in_specs=[HBM_SPEC],
        out_specs=VMEM_SPEC,
        scratch_shapes=held(couplings),
        compiler_params=pltpu.CompilerParams(vmem_limit_bytes=12 * 1024 * 1024),
        cost_estimate=pl.CostEstimate(flops=0, bytes_accessed=8000000, transcendentals=0),
        name="stage",
    )(pltpu.with_memory_space_constraint(couplings, pltpu.HBM))
    rounded = kernel_call(fold_kernel, "fold", folded(half), [tests])
    current, scale, folded_scale, places, far_slot = tests, None, None, None, None
    for sweep in range(SWEEPS):
        last = sweep == SWEEPS - 1
        before = shift(rounded, 1)
        after = shift(rounded, -1)
        if sweep == 0:
            rest, scale, folded_scale = kernel_call(
                first_center_kernel,
                "first_center",
                [
                    folded_whole,
                    jax.ShapeDtypeStruct((rows, width), F32),
                    jax.ShapeDtypeStruct((half, 2 * width), F32),
                ],
                [diag_blocks, current],
                held(diag_blocks),
            )
        else:
            rest = kernel_call(
                folded_center_kernel,
                "center",
                folded_whole,
                [diag_blocks, current, scale],
                held(diag_blocks) + [pltpu.VMEM((rows, vectors, width), F32)],
            )
        if sweep == 1:
            places = jnp.concatenate(
                [
                    from_block(before[half], SLOTS),
                    slot_aggs + SLAB_AGGS,
                    from_block(after[half], SLOTS) + 2 * SLAB_AGGS,
                ],
                axis=0,
            )
        part = kernel_call(
            couple_kernel,
            "couple",
            folded(half + last),
            [cols, couplings, before, rounded, after] + [slot_block] * last,
            [pltpu.VMEM((3 * rows, vectors, 2 * LANES), BF16)] * 2,
        )
        far = exchange(part, 0)
        if last:
            far_slot = from_block(far[half], stored)
        pair = kernel_call(pair_kernel, "pair", folded(half), [part, far])
        operands = [rest, pair, exchange(pair, 1), folded_scale]
        if last:
            current = kernel_call(last_update_kernel, "last_update", whole_shape, operands)
        else:
            current, rounded = kernel_call(
                update_kernel,
                "update",
                [folded_whole, folded(half + (sweep == 0))],
                operands + [ids_block] * (sweep == 0),
            )

    every = lax.all_gather(current, "vecs", axis=1, tiled=True)
    grams = jnp.einsum("ivb,iwb->ivw", every, every, precision=HIGHEST_PRECISION)
    members = (local_aggs[:, None] == jnp.arange(SLAB_AGGS, dtype=jnp.int32)[None, :]).astype(F32)
    totals = jnp.einsum("ig,ivw->vwg", members, grams, precision=HIGHEST_PRECISION) / width
    inverse = kernel_call(
        inverse_factor_kernel,
        "inverse_factor",
        jax.ShapeDtypeStruct((VECTORS, VECTORS, SLAB_AGGS), F32),
        [totals],
    )
    own_inverse = lax.dynamic_slice_in_dim(inverse, core * vectors, vectors, 0)
    row_inverse = jnp.einsum("ig,cvg->icv", members, own_inverse, precision=HIGHEST_PRECISION)
    tentative = jnp.einsum("icv,ivb->icb", row_inverse, every, precision=HIGHEST_PRECISION)

    moved = kernel_call(
        fit_kernel,
        "fit",
        jax.ShapeDtypeStruct((half, stored, vectors, 2 * width), BF16),
        [cols, couplings, tentative.astype(BF16)],
        [pltpu.VMEM((rows, vectors, 2 * LANES), BF16)] * 2,
    )
    rest = kernel_call(
        center_kernel,
        "center",
        folded_whole,
        [diag_blocks, tentative, scale],
        held(diag_blocks),
    )
    slots_shape = jax.ShapeDtypeStruct((half, SLOTS, vectors, 2 * width), BF16)
    pair = kernel_call(
        slot_kernel, "slots", slots_shape, [near_slot, far_slot, moved, exchange(moved, 0)]
    )
    prolong = kernel_call(
        finish_kernel, "finish", slots_shape, [rest, pair, exchange(pair, 1), folded_scale]
    )
    prolong_here = kernel_call(
        here_kernel,
        "here",
        jax.ShapeDtypeStruct((rows, 1, vectors, width), BF16),
        [where, prolong],
    )

    other = lax.ppermute(prolong, "vecs", [(0, 1), (1, 0)])
    before = shift(prolong, 1)
    after = shift(prolong, -1)
    span = 3 * SLAB_AGGS
    quarter = span * vectors // 4
    wide = SLAB_AGGS * 2 * vectors
    keep, send = kernel_call(
        coarse_kernel,
        "coarse",
        [
            jax.ShapeDtypeStruct((2, quarter, wide), F32),
            jax.ShapeDtypeStruct((2, quarter, wide), BF16),
        ],
        [where, cols, places, couplings, diag_blocks, before, prolong, after, other],
        [
            pltpu.VMEM((3 * rows, SLOTS, vectors, 2 * LANES), BF16),
            pltpu.VMEM((3 * rows, SLOTS, vectors, 2 * LANES), BF16),
            pltpu.VMEM((span, vectors, rows * 2 * LANES), BF16),
            pltpu.VMEM((2, SLAB_AGGS, vectors, rows * 2 * LANES), BF16),
            pltpu.VMEM((span * vectors, wide), F32),
        ]
        + [
            pltpu.VMEM((rows // 4, width, width), BF16),
            pltpu.SemaphoreType.DMA((1,)),
        ],
        limit=28,
    )
    merged = keep + exchange(send, 0).astype(F32)
    owned = merged[0] + exchange(merged[1].astype(BF16), 1).astype(F32)
    mine, theirs = owned[:, : wide // 2], owned[:, wide // 2 :]
    theirs = lax.ppermute(theirs, "vecs", [(0, 1), (1, 0)])
    low = jnp.where(core == 0, mine, theirs).reshape(span // 4, vectors, -1)
    high = jnp.where(core == 0, theirs, mine).reshape(span // 4, vectors, -1)
    coarse = jnp.concatenate([low, high], axis=1).reshape(span // 4, VECTORS, SLAB_AGGS, vectors)
    return (prolong_here, coarse.transpose(2, 0, 3, 1))


def solution(mesh):
    return jax.shard_map(
        on_device,
        mesh=mesh,
        in_specs=(
            P("rows", "aggs", None, None),
            P("rows", None, None),
            P("rows", "aggs"),
            P("rows"),
            P("rows", None),
            P("rows", "vecs", None),
        ),
        out_specs=(P("rows", "aggs", "vecs", None), P("rows", "aggs", "vecs", None)),
        check_vma=False,
    )
```
